768 devices in a mesh: panel: 2 (over x_hi), colat: 12 (over z), lon: 32 (over x_lo, y, core).
Axes of the slice: x: 4 (x_hi: 2, x_lo: 2; x = x_hi * 2 + x_lo), y: 8, z: 12, core: 2. Of those that a mesh axis runs over, the one named last changes fastest.
Arguments:
- fields: float32 [2, 8, 96, 288, 128], P('panel', None, 'colat', 'lon'), as said below
- donor_cell: int32 [2, 12, 64], P('panel', 'colat', 'lon'), may hold values from 0 to 61, as said below
- target_slot: int32 [2, 12, 64], P('panel', 'colat', 'lon'), may hold values from 0 to 13055, as said below
- donor_frac: float32 [2, 2, 12, 64], P('panel', None, 'colat', 'lon'), may hold values from 0 to 1
Outputs:
- increment: float32 [2, 8, 96, 288, 128], P('panel', None, 'colat', 'lon')
- section_input: float32 [2, 8, 96, 288, 128], P('panel', None, 'colat', 'lon')
The draws below stay inside these ranges and needn't reach their ends.
Inputs may be any that keep to these rules, and one draw needn't show every extreme that they name: `fields`: component 0 along the second dimension (density) lies between 0.5 and 2. `donor_cell`: each entry is a corner i * 9 + j of the donor device's own block with i <= 6 and j <= 7. `target_slot`: each of the 2 * (384) border points of a panel is named by exactly one slot of the other panel; the remaining slots hold -1.
All inputs are finite; a program needn't handle non-finite values.
Results may differ from the reference program's by a relative error of at most 0.00021.
Values sent between devices are 32-bit elements; how exact they have to be, the bound alone decides.
A program may use at most 32 MiB of HBM per device.

```python
import math
import jax
import jax.numpy as jnp
from jax import lax

CT = 8
CP = 9
NR = 128
NT = 96
NP = 288
KD = 2
N_COLAT = 12
N_LON = 32


def draw_fields(key, part):
    key = jax.random.fold_in(key, 11)
    dens_key, others_key = jax.random.split(key, 2)
    others_shape = (2, 7, NT, NP, NR)
    density = jnp.exp(jax.random.uniform(dens_key, (2, 1, NT, NP, NR), jnp.float32, math.log(0.5), math.log(2.0)))
    others = jnp.clip(jax.random.normal(others_key, others_shape, jnp.float32), -6.0, 6.0)
    return jnp.concatenate([density, others], axis=1).astype(jnp.float32)


def draw_donor_cell(key, part):
    key = jax.random.fold_in(key, 21)
    row_key, col_key = jax.random.split(key)
    row_pick = jax.random.randint(row_key, (2, N_COLAT, N_LON * KD), 0, CT - 1)
    col_pick = jax.random.randint(col_key, (2, N_COLAT, N_LON * KD), 0, CP - 1)
    corners = row_pick * CP + col_pick
    corners = corners.at[0, 0, 0].set((CT - 2) * CP + CP - 2).at[1, 0, 0].set(0)
    return corners.astype(jnp.int32)


def draw_target_slot(key, part):
    key = jax.random.fold_in(key, 31)
    rim_total = 2 * (CT + CP)
    border_total = 2 * (NT + NP)
    panels_out = []
    for panel_id in range(2):
        ordering = jax.random.permutation(jax.random.fold_in(key, panel_id), N_COLAT * N_LON * KD).astype(jnp.int32)
        upper_code = ordering // CP * rim_total + ordering % CP
        lower_off = ordering - NP
        lower_code = ((N_COLAT - 1) * N_LON + lower_off // CP) * rim_total + CP + lower_off % CP
        left_off = ordering - 2 * NP
        left_code = left_off // CT * N_LON * rim_total + 2 * CP + left_off % CT
        right_off = ordering - 2 * NP - NT
        right_code = (right_off // CT * N_LON + N_LON - 1) * rim_total + 2 * CP + CT + right_off % CT
        code_values = jnp.where(ordering < NP, upper_code, jnp.where(ordering < 2 * NP, lower_code, jnp.where(ordering < 2 * NP + NT, left_code, jnp.where(ordering < border_total, right_code, -1))))
        panels_out.append(code_values.reshape(N_COLAT, N_LON * KD))
    return jnp.stack(panels_out).astype(jnp.int32)


def level_of(stream_key, extent, cuts, smallest, top_value):
    factor_of, own = 1.0, jax.random.fold_in(stream_key, 6)
    for dim, parts in cuts:
        draws = jnp.exp(jax.random.uniform(jax.random.fold_in(own, dim), (parts,), jnp.float32, smallest / len(cuts), top_value / len(cuts)))
        factor_of = factor_of * jnp.repeat(draws, extent[dim] // parts).reshape([-1 if axis == dim else 1 for axis in range(len(extent))])
    return factor_of


def setup_inputs(seed: int = 0) -> dict:
    keys = jax.random.split(jax.random.key(seed), 5)
    return {
        "fields": draw_fields(jax.random.fold_in(keys[4], 71), 0),
        "donor_cell": draw_donor_cell(jax.random.fold_in(keys[4], 71), 0),
        "target_slot": draw_target_slot(jax.random.fold_in(keys[4], 71), 0),
        "donor_frac": jnp.clip(1.0 * jax.random.uniform(keys[3], (2, 2, N_COLAT, N_LON * KD), jnp.float32) ** level_of(keys[3], (2, 2, N_COLAT, N_LON * KD), ((0, 2), (2, 12), (3, 32)), -0.2, 0.2), 0.0, 1.0),
    }


GAMMA_GAS = 5.0 / 3.0
INNER_RADIUS = 0.35


def primitives(cells):
    density = cells[0]
    moment = cells[1:4]
    magnet = cells[4:7]
    energy = cells[7]
    velocity = moment / density
    magnet_square = jnp.sum(magnet * magnet, axis=0)
    pressure = (GAMMA_GAS - 1.0) * (energy - 0.5 * jnp.sum(moment * velocity, axis=0) - 0.5 * magnet_square)
    total_pressure = pressure + 0.5 * magnet_square
    alignment = jnp.sum(velocity * magnet, axis=0)
    return density, moment, magnet, energy, velocity, total_pressure, alignment


def directed(quantities, direction):
    density, moment, magnet, energy, velocity, total_pressure, alignment = quantities
    normal_speed = velocity[0] * direction[0] + velocity[1] * direction[1] + velocity[2] * direction[2]
    normal_field = magnet[0] * direction[0] + magnet[1] * direction[1] + magnet[2] * direction[2]
    components = [density * normal_speed]
    for component in range(3):
        components.append(moment[component] * normal_speed + total_pressure * direction[component] - magnet[component] * normal_field)
    for component in range(3):
        components.append(normal_speed * magnet[component] - normal_field * velocity[component])
    components.append((energy + total_pressure) * normal_speed - normal_field * alignment)
    return jnp.stack(components)


def tendency(padded, row_start, col_start, total_rows, total_cols):
    inner_rows = padded.shape[1] - 2
    inner_cols = padded.shape[2] - 2
    radial_count = padded.shape[3]
    step_theta = (0.5 * math.pi) / (total_rows - 3)
    step_phi = (1.5 * math.pi) / (total_cols - 3)
    step_radius = (1.0 - INNER_RADIUS) / (radial_count - 1)
    time_step = 0.3 * INNER_RADIUS * min(step_theta, step_phi)
    row_index = (row_start - 1 + jnp.arange(inner_rows + 2, dtype=jnp.int32)).astype(jnp.float32)
    col_index = (col_start - 1 + jnp.arange(inner_cols + 2, dtype=jnp.int32)).astype(jnp.float32)
    colatitude = 0.25 * math.pi + (row_index - 1.0) * step_theta
    longitude = -0.75 * math.pi + (col_index - 1.0) * step_phi
    radius = INNER_RADIUS + jnp.arange(radial_count, dtype=jnp.int32).astype(jnp.float32) * step_radius
    sine_theta = jnp.sin(colatitude)[:, None, None]
    cosine_theta = jnp.cos(colatitude)[:, None, None]
    sine_phi = jnp.sin(longitude)[None, :, None]
    cosine_phi = jnp.cos(longitude)[None, :, None]
    radius_grid = radius[None, None, :]
    mid_st = sine_theta[1:-1]
    mid_ct = cosine_theta[1:-1]
    mid_sp = sine_phi[:, 1:-1]
    mid_cp = cosine_phi[:, 1:-1]
    inner_parts = primitives(padded[:, 1:-1, 1:-1])
    flux_radial = directed(inner_parts, (mid_st * mid_cp, mid_st * mid_sp, mid_ct))
    flux_polar_mid = directed(inner_parts, (mid_ct * mid_cp, mid_ct * mid_sp, -mid_st))
    flux_azimuth_mid = directed(inner_parts, (-mid_sp, mid_cp, 0.0))
    edge_rows = padded[:, 0::inner_rows + 1, 1:-1]
    edge_st = sine_theta[0::inner_rows + 1]
    edge_ct = cosine_theta[0::inner_rows + 1]
    flux_polar_edge = directed(primitives(edge_rows), (edge_ct * mid_cp, edge_ct * mid_sp, -edge_st))
    edge_cols = padded[:, 1:-1, 0::inner_cols + 1]
    edge_sp = sine_phi[:, 0::inner_cols + 1]
    edge_cp = cosine_phi[:, 0::inner_cols + 1]
    flux_azimuth_edge = directed(primitives(edge_cols), (-edge_sp, edge_cp, 0.0))
    flux_polar = jnp.concatenate([flux_polar_edge[:, :1], flux_polar_mid, flux_polar_edge[:, 1:]], axis=1)
    flux_azimuth = jnp.concatenate([flux_azimuth_edge[:, :, :1], flux_azimuth_mid, flux_azimuth_edge[:, :, 1:]], axis=2)
    weighted = sine_theta * flux_polar
    polar_term = (weighted[:, 2:] - weighted[:, :-2]) / (2.0 * step_theta)
    azimuth_term = (flux_azimuth[:, :, 2:] - flux_azimuth[:, :, :-2]) / (2.0 * step_phi)
    angular = (polar_term + azimuth_term) / (radius_grid * mid_st)
    squared = radius_grid * radius_grid
    scaled = squared * flux_radial
    radial = (scaled[..., 2:] - scaled[..., :-2]) / (2.0 * step_radius) / squared[..., 1:-1]
    radial = jnp.pad(radial, ((0, 0), (0, 0), (0, 0), (1, 1)))
    position = jnp.arange(radial_count, dtype=jnp.int32)
    interior = (position > 0) & (position < radial_count - 1)
    return jnp.where(interior, -time_step * (angular + radial), 0.0).astype(jnp.float32)


def donate(flattened, corner, stride, weight_row, weight_col):
    anchor = flattened[:, corner]
    lower_cell = flattened[:, corner + stride]
    beside = flattened[:, corner + 1]
    across = flattened[:, corner + stride + 1]
    share_row = weight_row[None, :, None]
    share_col = weight_col[None, :, None]
    blended = (1.0 - share_row) * (1.0 - share_col) * anchor + share_row * (1.0 - share_col) * lower_cell + (1.0 - share_row) * share_col * beside + share_row * share_col * across
    return jnp.stack([blended[0], -blended[1], blended[3], blended[2], -blended[4], blended[6], blended[5], blended[7]])


def ghost_place(code_list):
    rim_total = 2 * (CT + CP)
    filled = code_list >= 0
    device = code_list // rim_total
    rim_slot = code_list % rim_total
    colat_dev = device // N_LON
    lon_dev = device % N_LON
    upper_row = rim_slot < CP
    lower_row = (rim_slot >= CP) & (rim_slot < 2 * CP)
    left_col = (rim_slot >= 2 * CP) & (rim_slot < 2 * CP + CT)
    ghost_row = jnp.where(upper_row, 0, jnp.where(lower_row, NT + 1, 1 + colat_dev * CT + jnp.where(left_col, rim_slot - 2 * CP, rim_slot - 2 * CP - CT)))
    ghost_col = jnp.where(upper_row, 1 + lon_dev * CP + rim_slot, jnp.where(lower_row, 1 + lon_dev * CP + rim_slot - CP, jnp.where(left_col, 0, NP + 1)))
    ghost_row = jnp.where(filled, ghost_row, NT + 5)
    return ghost_row.astype(jnp.int32), ghost_col.astype(jnp.int32)


def reference(fields, donor_cell, target_slot, donor_frac):
    increments = []
    sections = []
    for target in range(2):
        source = 1 - target
        flattened = fields[source].reshape(8, NT * NP, NR)
        corners = donor_cell[source].reshape(-1)
        slot_index = jnp.arange(corners.shape[0], dtype=jnp.int32)
        colat_dev = slot_index // (N_LON * KD)
        lon_dev = (slot_index % (N_LON * KD)) // KD
        corner = ((colat_dev * CT + corners // CP) * NP + lon_dev * CP + corners % CP).astype(jnp.int32)
        packets = donate(flattened, corner, NP, donor_frac[source, 0].reshape(-1), donor_frac[source, 1].reshape(-1))
        ghost_row, ghost_col = ghost_place(target_slot[source].reshape(-1))
        padded = jnp.pad(fields[target], ((0, 0), (1, 1), (1, 1), (0, 0)))
        padded = padded.at[:, ghost_row, ghost_col, :].set(packets, mode="drop")

        def one_block(block_id):
            block = lax.dynamic_slice_in_dim(padded, block_id * CT, CT + 2, axis=1)
            return tendency(block, block_id * CT, 0, NT, NP)

        blocks = lax.map(one_block, jnp.arange(N_COLAT, dtype=jnp.int32))
        increment = jnp.transpose(blocks, (1, 0, 2, 3, 4)).reshape(8, NT, NP, NR)
        increments.append(increment)
        sections.append(fields[target] + 0.5 * increment)
    return jnp.stack(increments), jnp.stack(sections)
```

```python
import functools
import math

import jax
import jax.numpy as jnp
from jax import lax
from jax.experimental import pallas as pl
from jax.experimental.pallas import tpu as pltpu
from jax.sharding import PartitionSpec as P

GAMMA_GAS = 5.0 / 3.0
INNER_RADIUS = 0.35
MESH = pl.DeviceIdType.MESH
ROWS, COLS, RADII = 8, 9, 128
COLAT, LON, CHIPS = 12, 32, 16
RIM = 2 * (ROWS + COLS)
F32 = jnp.float32

STEP_THETA = 0.5 * math.pi / (ROWS * COLAT - 3)
STEP_PHI = 1.5 * math.pi / (COLS * LON - 3)
STEP_RADIUS = (1.0 - INNER_RADIUS) / (RADII - 1)
TIME_STEP = 0.3 * INNER_RADIUS * min(STEP_THETA, STEP_PHI)
FRAME = ((0, 1.0), (1, -1.0), (3, 1.0), (2, 1.0), (4, -1.0), (6, 1.0), (5, 1.0), (7, 1.0))


def primitives(q):
    inverse = 1.0 / q[0]
    v = [q[1] * inverse, q[2] * inverse, q[3] * inverse]
    magnet = q[4] * q[4] + q[5] * q[5] + q[6] * q[6]
    motion = q[1] * v[0] + q[2] * v[1] + q[3] * v[2]
    total = (GAMMA_GAS - 1.0) * (q[7] - 0.5 * motion - 0.5 * magnet) + 0.5 * magnet
    alignment = v[0] * q[4] + v[1] * q[5] + v[2] * q[6]
    return v, total, alignment


def flux(q, prim, d):
    v, total, alignment = prim
    vd = v[0] * d[0] + v[1] * d[1]
    bd = q[4] * d[0] + q[5] * d[1]
    if d[2] is not None:
        vd = vd + v[2] * d[2]
        bd = bd + q[6] * d[2]
    out = [q[0] * vd]
    for a in range(3):
        term = q[1 + a] * vd - q[4 + a] * bd
        if d[a] is not None:
            term = term + total * d[a]
        out.append(term)
    for a in range(3):
        out.append(vd * q[4 + a] - bd * v[a])
    out.append((q[7] + total) * vd - bd * alignment)
    return out


def owner_of(code):
    code0 = jnp.maximum(code, 0)
    device, slot = lax.div(code0, RIM), lax.rem(code0, RIM)
    c, l = lax.div(device, LON), lax.rem(device, LON)
    side = jnp.where(slot < 26, c * 8 + slot - 18, 96 + c * 8 + slot - 26)
    side = jnp.maximum(side, 0)
    level = jnp.where(slot < 9, slot, jnp.where(slot < 18, slot + 6, 9 + lax.rem(side, 6)))
    column = jnp.where(slot < 18, l, lax.div(side, 6))
    return jnp.where(code < 0, -1, level * LON + column)


def slot_goal(c, l, s):
    level = 2 * c + s
    v = l * 6 + jnp.maximum(level - 9, 0)
    top, bottom, left = level < 9, level >= 15, v < 96
    row = jnp.where(left, v // 8, (v - 96) // 8)
    goal_c = jnp.where(top, 0, jnp.where(bottom, COLAT - 1, row))
    goal_l = jnp.where(top | bottom, l, jnp.where(left, 0, LON - 1))
    slot = jnp.where(top, level, jnp.where(bottom, level - 6, jnp.where(left, 18 + v % 8, 26 + v % 8)))
    kind = jnp.where(top, 0, jnp.where(bottom, 1, jnp.where(left, 2, 3)))
    return goal_c, goal_l, slot, kind


def kernel(fields, cells, targets, frac, inc_out, sec_out,
           state, gather, sends, parts, collected, rim, top, bottom, left, right,
           trig, azimuth, inc, sec,
           load_sem, zs, zr, cs, cr, as_, ar, fs, fr, hs, hr, out_sem):
    p, c, l = lax.axis_index("panel"), lax.axis_index("colat"), lax.axis_index("lon")
    core, chip = l % 2, l // 2
    is_top, is_bottom, is_left, is_right = c == 0, c == COLAT - 1, l == 0, l == LON - 1

    def remote(src, dst, send, recv, device):
        return pltpu.make_async_remote_copy(
            src_ref=src, dst_ref=dst, send_sem=send, recv_sem=recv,
            device_id=device, device_id_type=MESH)

    load = pltpu.make_async_copy(fields, state, load_sem)
    load.start()

    barrier = pltpu.get_barrier_semaphore()

    def greet(device):
        pl.semaphore_signal(barrier, inc=1, device_id=device, device_id_type=MESH)

    for k in range(1, COLAT):
        greet((p, (c + k) % COLAT, l))
    for k in range(1, CHIPS):
        greet((p, c, (chip + k) % CHIPS * 2 + core))
    pl.when(l > 0)(lambda: greet((p, c, l - 1)))
    pl.when(l < LON - 1)(lambda: greet((p, c, l + 1)))

    @pl.when(is_top)
    def _():
        for k in range(9):
            greet((1 - p, k // 2, l))

    @pl.when(is_bottom)
    def _():
        for k in range(9):
            greet((1 - p, (15 + k) // 2, l))

    @pl.when(is_left)
    def _():
        for k in range(8):
            v = c * 8 + k
            greet((1 - p, (9 + v % 6) // 2, v // 6))

    @pl.when(is_right)
    def _():
        for k in range(8):
            v = 96 + c * 8 + k
            greet((1 - p, (9 + v % 6) // 2, v // 6))

    load.wait()
    for s in range(2):
        cell = cells[0, 0, s]
        i, j = lax.div(cell, COLS), lax.rem(cell, COLS)
        a, b = frac[0, 0, 0, s], frac[0, 1, 0, s]
        weights = ((1.0 - a) * (1.0 - b), a * (1.0 - b), (1.0 - a) * b, a * b)
        values = []
        for q in range(8):
            corners = (state[q, j, pl.ds(i, 1), :], state[q, j, pl.ds(i + 1, 1), :],
                       state[q, j + 1, pl.ds(i, 1), :], state[q, j + 1, pl.ds(i + 1, 1), :])
            value = weights[0] * corners[0]
            for w in range(1, 4):
                value = value + weights[w] * corners[w]
            values.append(value)
        for place, (q, sign) in enumerate(FRAME):
            gather[core, c, s * 8 + place : s * 8 + place + 1, :] = values[q] if sign > 0 else -values[q]
        gather[core, c, 16 + s : 17 + s, :] = jnp.full((1, RADII), owner_of(targets[0, 0, s]).astype(F32), F32)

    pl.semaphore_wait(barrier, 11 + 15 + 2 + jnp.where(is_left | is_right, 1, 2))

    def bundle(at_core, z):
        return gather.at[at_core, z, pl.ds(0, 18), :]

    z_copies = []
    for k in (6, 5, 7, 4, 8, 3, 9, 2, 10, 1, 11):
        copy = remote(bundle(core, c), bundle(core, c), zs.at[k], zr.at[c], (p, (c + k) % COLAT, l))
        copy.start()
        z_copies.append(copy)

    to_right = remote(state.at[:, COLS - 1], left, hs.at[2], hr.at[2], (p, c, l + 1))
    to_left = remote(state.at[:, 0], right, hs.at[3], hr.at[3], (p, c, l - 1))
    to_below = remote(state.at[:, :, ROWS - 1, :], top, hs.at[0], hr.at[0], (p, c + 1, l))
    to_above = remote(state.at[:, :, 0, :], bottom, hs.at[1], hr.at[1], (p, c - 1, l))
    pl.when(l < LON - 1)(to_right.start)
    pl.when(l > 0)(to_left.start)

    index = lax.broadcasted_iota(jnp.int32, (16, RADII), 0)
    theta = 0.25 * math.pi + ((c * ROWS - 1 + index).astype(F32) - 1.0) * STEP_THETA
    phi = -0.75 * math.pi + ((l * COLS - 1 + index).astype(F32) - 1.0) * STEP_PHI
    trig[0] = jnp.sin(theta)
    trig[1] = jnp.cos(theta)
    trig[2] = jnp.sin(phi)
    trig[3] = jnp.cos(phi)
    lane = lax.broadcasted_iota(jnp.int32, (ROWS, RADII), 1)
    row = lax.broadcasted_iota(jnp.int32, (ROWS, RADII), 0)
    radius = INNER_RADIUS + lane.astype(F32) * STEP_RADIUS
    square = radius * radius
    st, ct = trig[0, 1 : 1 + ROWS, :], trig[1, 1 : 1 + ROWS, :]
    angular = -TIME_STEP / (radius * st)
    k_theta = angular * (1.0 / (2.0 * STEP_THETA))
    k_phi = angular * (1.0 / (2.0 * STEP_PHI))
    k_radius = -TIME_STEP / (2.0 * STEP_RADIUS) / square
    k_below = jnp.where(row == ROWS - 1, 0.0, k_theta)
    k_above = jnp.where(row == 0, 0.0, k_theta)
    k_bottom = jnp.where(row == ROWS - 1, k_theta, 0.0)
    k_top = jnp.where(row == 0, k_theta, 0.0)
    inside = (lane > 0) & (lane < RADII - 1)

    def column(j, carry):
        q = [state[n, j] for n in range(8)]
        sp, cp = trig[2, pl.ds(j + 1, 1), :], trig[3, pl.ds(j + 1, 1), :]
        prim = primitives(q)
        f_r = flux(q, prim, (st * cp, st * sp, ct))
        f_t = flux(q, prim, (ct * cp, ct * sp, -st))
        f_p = flux(q, prim, (-sp, cp, None))
        for n in range(8):
            weighted = square * f_r[n]
            value = k_radius * (pltpu.roll(weighted, RADII - 1, 1) - pltpu.roll(weighted, 1, 1))
            slanted = st * f_t[n]
            value = value + k_below * pltpu.roll(slanted, ROWS - 1, 0) - k_above * pltpu.roll(slanted, 1, 0)
            inc[n, j] = value
            azimuth[n, j + 1] = f_p[n]
        return carry

    lax.fori_loop(0, COLS, column, 0)

    for z in range(COLAT):
        @pl.when(c != z)
        def _():
            remote(bundle(core, z), bundle(core, z), zs.at[0], zr.at[z], (p, c, l)).wait_recv()

    pl.when(c < COLAT - 1)(to_below.start)
    pl.when(c > 0)(to_above.start)
    twin = l + 1 - 2 * core
    share = remote(gather.at[core], gather.at[core], cs.at[0], cr.at[0], (p, c, twin))
    share.start()
    remote(gather.at[1 - core], gather.at[1 - core], cs.at[0], cr.at[0], (p, c, twin)).wait_recv()

    offset = (2 * c * LON + core).astype(F32)

    def pick(n, sums):
        sums = list(sums)
        at_core, z = n // COLAT, n % COLAT
        for s in range(2):
            value = gather[at_core, z, s * 8 : s * 8 + 8, :]
            number = jnp.broadcast_to(gather[at_core, z, 16 + s : 17 + s, :] - offset, (8, RADII))
            for t in range(32):
                goal = float(t % 2 * LON + t // 2 * 2)
                sums[t] = jnp.where(number == goal, value, sums[t])
        return tuple(sums)

    sums = lax.fori_loop(0, 2 * COLAT, pick, tuple(jnp.zeros((8, RADII), F32) for _ in range(32)))
    for t in range(32):
        sends[t // 2, t % 2 * 8 : t % 2 * 8 + 8, :] = sums[t]

    a_copies = []
    for k in range(1, CHIPS):
        goal = (chip + k) % CHIPS
        copy = remote(sends.at[goal], parts.at[k], as_.at[k], ar.at[k], (p, c, goal * 2 + core))
        copy.start()
        a_copies.append(copy)
    total = sends[chip]
    for k in range(1, CHIPS):
        a_copies[k - 1].wait_recv()
        total = total + parts[k]
    collected[...] = total

    f_copies = []
    for s in range(2):
        goal_c, goal_l, slot, kind = slot_goal(c, l, s)
        copy = remote(collected.at[pl.ds(s * 8, 8), :], rim.at[pl.ds(pl.multiple_of(slot * 8, 8), 8), :],
                      fs.at[s], fr.at[kind], (1 - p, goal_c, goal_l))
        copy.start()
        f_copies.append(copy)

    def edge(border, kind, copy_in, buffer, first, count):
        @pl.when(jnp.logical_not(border))
        def _():
            copy_in.wait_recv()

        @pl.when(border)
        def _():
            window = rim.at[pl.ds(first * 8, count * 8), :]
            remote(window, window, fs.at[0], fr.at[kind], (p, c, l)).wait_recv()
            for n in range(8):
                buffer[n] = rim[pl.ds(first * 8 + n, count, stride=8), :]

    edge(is_top, 0, to_below, top, 0, 9)
    edge(is_bottom, 1, to_above, bottom, 9, 9)
    edge(is_left, 2, to_right, left, 18, 8)
    edge(is_right, 3, to_left, right, 26, 8)
    sp, cp = trig[2, 1 : 1 + COLS, :], trig[3, 1 : 1 + COLS, :]
    for buffer, at in ((top, 0), (bottom, ROWS + 1)):
        q = [buffer[n] for n in range(8)]
        edge_st, edge_ct = trig[0, at : at + 1, :], trig[1, at : at + 1, :]
        f_t = flux(q, primitives(q), (edge_ct * cp, edge_ct * sp, -edge_st))
        for n in range(8):
            buffer[n] = edge_st * f_t[n]
    for buffer, at in ((left, 0), (right, COLS + 1)):
        q = [buffer[n] for n in range(8)]
        f_p = flux(q, primitives(q), (-trig[2, at : at + 1, :], trig[3, at : at + 1, :], None))
        for n in range(8):
            azimuth[n, at] = f_p[n]

    outs = []
    for j in range(COLS):
        for n in range(8):
            value = inc[n, j] + k_phi * (azimuth[n, j + 2] - azimuth[n, j])
            value = value + k_bottom * bottom[n, j : j + 1, :] - k_top * top[n, j : j + 1, :]
            value = jnp.where(inside, value, 0.0)
            inc[n, j] = value
            sec[n, j] = state[n, j] + 0.5 * value
        for which, (source, goal) in enumerate(((inc, inc_out), (sec, sec_out))):
            copy = pltpu.make_async_copy(source.at[:, j], goal.at[:, j], out_sem.at[which, j])
            copy.start()
            outs.append(copy)

    for copy in z_copies + [share] + a_copies + f_copies:
        copy.wait_send()
    pl.when(c < COLAT - 1)(to_below.wait_send)
    pl.when(c > 0)(to_above.wait_send)
    pl.when(l < LON - 1)(to_right.wait_send)
    pl.when(l > 0)(to_left.wait_send)
    for copy in outs:
        copy.wait()


def shards(fields, donor_cell, target_slot, donor_frac):
    hbm, smem = pl.BlockSpec(memory_space=pl.ANY), pl.BlockSpec(memory_space=pltpu.SMEM)
    vmem, dma = pltpu.VMEM, pltpu.SemaphoreType.DMA
    shape = jax.ShapeDtypeStruct((8, COLS, ROWS, RADII), F32)
    increment, sectioned = pl.pallas_call(
        kernel,
        out_shape=(shape, shape),
        in_specs=[hbm, smem, smem, smem],
        out_specs=(hbm, hbm),
        scratch_shapes=[
            vmem((8, COLS, ROWS, RADII), F32),
            vmem((2, COLAT, 24, RADII), F32),
            vmem((CHIPS, 16, RADII), F32),
            vmem((CHIPS, 16, RADII), F32),
            vmem((16, RADII), F32),
            vmem((RIM * 8, RADII), F32),
            vmem((8, COLS, RADII), F32),
            vmem((8, COLS, RADII), F32),
            vmem((8, ROWS, RADII), F32),
            vmem((8, ROWS, RADII), F32),
            vmem((4, 16, RADII), F32),
            vmem((8, COLS + 2, ROWS, RADII), F32),
            vmem((8, COLS, ROWS, RADII), F32),
            vmem((8, COLS, ROWS, RADII), F32),
            dma, dma((COLAT,)), dma((COLAT,)), dma((1,)), dma((1,)),
            dma((CHIPS,)), dma((CHIPS,)), dma((2,)), dma((4,)), dma((4,)), dma((4,)), dma((2, COLS)),
        ],
        compiler_params=pltpu.CompilerParams(collective_id=0, has_side_effects=True),
        cost_estimate=pl.CostEstimate(flops=30_000_000, bytes_accessed=2_000_000, transcendentals=0),
    )(jnp.transpose(fields[0], (0, 2, 1, 3)), donor_cell, target_slot, donor_frac)
    return tuple(jnp.transpose(x, (0, 2, 1, 3))[None] for x in (increment, sectioned))


def solution(mesh):
    placed = (
        P("panel", None, "colat", "lon", None),
        P("panel", "colat", "lon"),
        P("panel", "colat", "lon"),
        P("panel", None, "colat", "lon"),
    )
    return jax.shard_map(
        shards,
        mesh=mesh,
        in_specs=placed,
        out_specs=(P("panel", None, "colat", "lon", None), P("panel", None, "colat", "lon", None)),
        check_vma=False,
    )
```

```python
import functools
import math

import jax
import jax.numpy as jnp
from jax import lax
from jax.experimental import pallas as pl
from jax.experimental.pallas import tpu as pltpu
from jax.sharding import PartitionSpec as P

GAMMA_GAS = 5.0 / 3.0
INNER_RADIUS = 0.35
MESH = pl.DeviceIdType.MESH
ROWS, COLS, RADII = 8, 9, 128
COLAT, LON, RING, CHIPS = 12, 32, 8, 16
RIM = 2 * (ROWS + COLS)
EARLY, UPPER, CLASS = 6, 3, 80
ORDER = (4, 12, 3, 5, 11, 13, 6, 2, 10, 14, 7, 1, 9, 15, 8, 0)
NEAR = (0, 8, 7, 15)
F32 = jnp.float32

STEP_THETA = 0.5 * math.pi / (ROWS * COLAT - 3)
STEP_PHI = 1.5 * math.pi / (COLS * LON - 3)
STEP_RADIUS = (1.0 - INNER_RADIUS) / (RADII - 1)
TIME_STEP = 0.3 * INNER_RADIUS * min(STEP_THETA, STEP_PHI)
FRAME = ((0, 1.0), (1, -1.0), (3, 1.0), (2, 1.0), (4, -1.0), (6, 1.0), (5, 1.0), (7, 1.0))


def primitives(q):
    inverse = 1.0 / q[0]
    v = [q[1] * inverse, q[2] * inverse, q[3] * inverse]
    magnet = q[4] * q[4] + q[5] * q[5] + q[6] * q[6]
    motion = q[1] * v[0] + q[2] * v[1] + q[3] * v[2]
    total = (GAMMA_GAS - 1.0) * (q[7] - 0.5 * motion - 0.5 * magnet) + 0.5 * magnet
    alignment = v[0] * q[4] + v[1] * q[5] + v[2] * q[6]
    return v, total, alignment


def flux(q, prim, d):
    v, total, alignment = prim
    vd = v[0] * d[0] + v[1] * d[1]
    bd = q[4] * d[0] + q[5] * d[1]
    if d[2] is not None:
        vd = vd + v[2] * d[2]
        bd = bd + q[6] * d[2]
    out = [q[0] * vd]
    for a in range(3):
        term = q[1 + a] * vd - q[4 + a] * bd
        if d[a] is not None:
            term = term + total * d[a]
        out.append(term)
    for a in range(3):
        out.append(vd * q[4 + a] - bd * v[a])
    out.append((q[7] + total) * vd - bd * alignment)
    return out


def owner_of(code):
    code0 = jnp.maximum(code, 0)
    device, slot = lax.div(code0, RIM), lax.rem(code0, RIM)
    c, l = lax.div(device, LON), lax.rem(device, LON)
    is_right = jnp.where(slot >= 26, 1, 0)
    w = jnp.maximum(slot - 18 - 8 * is_right, 0)
    near = c < EARLY
    v = jnp.maximum(c - EARLY, 0) * 16 + is_right * 8 + w
    is_row = slot < 18
    lon = jnp.where(is_row, l, lax.rem(v, LON))
    spot = jnp.where(is_row, lax.rem(slot, 3), 3)
    place = lax.div(lon, 2) * 4 + spot
    core = lax.rem(lon, 2)
    plane = jnp.where(is_row, lax.div(slot, 3), UPPER + lax.div(v, LON))
    at_side = near & jnp.logical_not(is_row)
    plane = jnp.where(at_side, c, plane)
    place = jnp.where(at_side, 64 + is_right * 4 + lax.div(w, 4) * 2 + lax.rem(w, 2), place)
    core = jnp.where(at_side, lax.rem(lax.div(w, 2), 2), core)
    return jnp.where(code < 0, -1, (plane * 2 + core) * CLASS + place)


def far_side_goal(c, l):
    v = (c - UPPER) * LON + l
    is_right = v % 16 // 8
    return EARLY + v // 16, is_right * (LON - 1), 18 + is_right * 8 + v % 8


def kernel(fields, cells_in, targets_in, frac_in, inc, sec,
           cells, targets, frac, state, mine, gather, sends, near_sends, parts, near_parts, collected, near_collected, rim, top, bottom, left, right,
           trig, azimuth, load_sem, zs, zr, ts, tr, as_, ar, ns, nr, fs, fr, gs, gr, ms, mr, hs, hr, ready):
    p, c, l = lax.axis_index("panel"), lax.axis_index("colat"), lax.axis_index("lon")
    core, x, y = l % 2, l // 16, l // 2 % RING
    chip = l // 2
    is_top, is_bottom, is_left, is_right = c == 0, c == COLAT - 1, l == 0, l == LON - 1
    early, upper = c < EARLY, c < UPPER
    middle = early & jnp.logical_not(upper)
    late = jnp.logical_not(early)
    is_side = is_left | is_right

    def remote(src, dst, send, recv, device):
        return pltpu.make_async_remote_copy(
            src_ref=src, dst_ref=dst, send_sem=send, recv_sem=recv,
            device_id=device, device_id_type=MESH)

    loads = [pltpu.make_async_copy(source, goal, load_sem.at[i])
             for i, (source, goal) in enumerate(((fields, state), (cells_in, cells), (targets_in, targets), (frac_in, frac)))]
    for load in loads:
        load.start()

    barrier = pltpu.get_barrier_semaphore()

    def greet(device):
        pl.semaphore_signal(barrier, inc=1, device_id=device, device_id_type=MESH)

    pl.when(l > 0)(lambda: greet((p, c, l - 1)))
    pl.when(l < LON - 1)(lambda: greet((p, c, l + 1)))

    pl.when(c > 0)(lambda: greet((p, c - 1, l)))
    pl.when(c < COLAT - 1)(lambda: greet((p, c + 1, l)))
    across = (1 - x) * 16 + y * 2

    @pl.when(early)
    def _():
        for k in range(COLAT):
            greet((1 - p, (c + 6 + k) % COLAT, across + core))
        for k in range(1, CHIPS):
            greet((p, c, (chip + k) % CHIPS * 2 + core))

    pl.when(early & is_left)(lambda: greet((p, c, 17)))
    pl.when(early & is_right)(lambda: greet((p, c, 14)))
    pl.when(is_top)(lambda: greet((p, 2, l)))

    @pl.when(middle)
    def _():
        greet((p, COLAT - 1, l))
        goal_c, goal_l, _ = far_side_goal(c, l)
        greet((p, goal_c, goal_l))

    for load in loads:
        load.wait()
    for s in range(2):
        cell = cells[0, 0, s]
        i, j = lax.div(cell, COLS), lax.rem(cell, COLS)
        a, b = frac[0, 0, 0, s], frac[0, 1, 0, s]
        weights = ((1.0 - a) * (1.0 - b), a * (1.0 - b), (1.0 - a) * b, a * b)
        values = []
        for q in range(8):
            corners = (state[q, j, pl.ds(i, 1), :], state[q, j, pl.ds(i + 1, 1), :],
                       state[q, j + 1, pl.ds(i, 1), :], state[q, j + 1, pl.ds(i + 1, 1), :])
            value = weights[0] * corners[0]
            for w in range(1, 4):
                value = value + weights[w] * corners[w]
            values.append(value)
        for place, (q, sign) in enumerate(FRAME):
            mine[s * 8 + place : s * 8 + place + 1, :] = values[q] if sign > 0 else -values[q]
        mine[16 + s : 17 + s, :] = jnp.full((1, RADII), owner_of(targets[0, 0, s]).astype(F32), F32)

    pl.semaphore_wait(
        barrier,
        EARLY
        + jnp.where(is_top | is_bottom, 1, 2)
        + jnp.where(is_side, 1, 2)
        + jnp.where(early, CHIPS - 1, 0)
        + jnp.where(early & ((l == 17) | (l == 14)), 1, 0)
        + jnp.where(c == 2, 1, 0)
        + jnp.where(is_bottom, EARLY - UPPER, 0)
        + jnp.where(late & is_side, 8, 0),
    )

    def bundle(at_group, z):
        return gather.at[at_group, z, pl.ds(0, 18), :]

    turned_c = (c + 1) % COLAT
    z_copies = [
        remote(mine.at[pl.ds(0, 18), :], bundle(core, turned_c), zs.at[k], zr.at[turned_c], (1 - p, k, across + core))
        for k in range(EARLY)
    ]
    for copy in z_copies:
        copy.start()

    def six(at_core, part):
        return gather.at[at_core, pl.ds(part * 6, 6), pl.ds(0, 18), :]

    def over(part):
        return remote(six(core, part), six(core, part), ts.at[part], tr.at[part], (p, c, l + 1 - 2 * core))

    to_right = remote(state.at[:, COLS - 1], left, hs.at[2], hr.at[2], (p, c, l + 1))
    to_left = remote(state.at[:, 0], right, hs.at[3], hr.at[3], (p, c, l - 1))
    to_below = remote(state.at[:, :, ROWS - 1, :], top, hs.at[0], hr.at[0], (p, c + 1, l))
    to_above = remote(state.at[:, :, 0, :], bottom, hs.at[1], hr.at[1], (p, c - 1, l))
    pl.when(l < LON - 1)(to_right.start)
    pl.when(l > 0)(to_left.start)
    pl.when(c < COLAT - 1)(to_below.start)
    pl.when(c > 0)(to_above.start)

    def announce(device):
        pl.semaphore_signal(ready, inc=1, device_id=device, device_id_type=MESH)

    @pl.when(is_bottom)
    def _():
        for k in range(UPPER, EARLY):
            announce((p, k, l))

    @pl.when(late & is_side)
    def _():
        for k in range(8):
            v = (c - EARLY) * 16 + jnp.where(is_right, 8, 0) + k
            announce((p, UPPER + v // LON, v % LON))

    index = lax.broadcasted_iota(jnp.int32, (16, RADII), 0)
    theta = 0.25 * math.pi + ((c * ROWS - 1 + index).astype(F32) - 1.0) * STEP_THETA
    phi = -0.75 * math.pi + ((l * COLS - 1 + index).astype(F32) - 1.0) * STEP_PHI
    trig[0] = jnp.sin(theta)
    trig[1] = jnp.cos(theta)
    trig[2] = jnp.sin(phi)
    trig[3] = jnp.cos(phi)
    lane = lax.broadcasted_iota(jnp.int32, (ROWS, RADII), 1)
    row = lax.broadcasted_iota(jnp.int32, (ROWS, RADII), 0)
    radius = INNER_RADIUS + lane.astype(F32) * STEP_RADIUS
    square = radius * radius
    st, ct = trig[0, 1 : 1 + ROWS, :], trig[1, 1 : 1 + ROWS, :]
    angular = -TIME_STEP / (radius * st)
    k_theta = angular * (1.0 / (2.0 * STEP_THETA))
    k_phi = angular * (1.0 / (2.0 * STEP_PHI))
    k_radius = -TIME_STEP / (2.0 * STEP_RADIUS) / square
    k_below = jnp.where(row == ROWS - 1, 0.0, k_theta)
    k_above = jnp.where(row == 0, 0.0, k_theta)
    k_bottom = jnp.where(row == ROWS - 1, k_theta, 0.0)
    k_top = jnp.where(row == 0, k_theta, 0.0)
    inside = (lane > 0) & (lane < RADII - 1)

    def column(j, carry):
        q = [state[n, j] for n in range(8)]
        sp, cp = trig[2, pl.ds(j + 1, 1), :], trig[3, pl.ds(j + 1, 1), :]
        prim = primitives(q)
        f_r = flux(q, prim, (st * cp, st * sp, ct))
        f_t = flux(q, prim, (ct * cp, ct * sp, -st))
        f_p = flux(q, prim, (-sp, cp, None))
        for n in range(8):
            weighted = square * f_r[n]
            value = k_radius * (pltpu.roll(weighted, RADII - 1, 1) - pltpu.roll(weighted, 1, 1))
            slanted = st * f_t[n]
            value = value + k_below * pltpu.roll(slanted, ROWS - 1, 0) - k_above * pltpu.roll(slanted, 1, 0)
            inc[n, j] = value
            azimuth[n, j + 1] = f_p[n]
        return carry

    lax.fori_loop(0, COLS, column, 0)

    def row_edge(buffer, at):
        q = [buffer[n] for n in range(8)]
        sp, cp = trig[2, 1 : 1 + COLS, :], trig[3, 1 : 1 + COLS, :]
        edge_st, edge_ct = trig[0, at : at + 1, :], trig[1, at : at + 1, :]
        f_t = flux(q, primitives(q), (edge_ct * cp, edge_ct * sp, -edge_st))
        for n in range(8):
            buffer[n] = edge_st * f_t[n]

    def column_edge(buffer, at):
        q = [buffer[n] for n in range(8)]
        f_p = flux(q, primitives(q), (-trig[2, at : at + 1, :], trig[3, at : at + 1, :], None))
        for n in range(8):
            azimuth[n, at] = f_p[n]

    sides = (
        (is_top, to_below, top, row_edge, 0, 0, 9),
        (is_bottom, to_above, bottom, row_edge, ROWS + 1, 9, 9),
        (is_left, to_right, left, column_edge, 0, 18, 8),
        (is_right, to_left, right, column_edge, COLS + 1, 26, 8),
    )
    for border, copy_in, buffer, work, at, first, count in sides:
        @pl.when(jnp.logical_not(border))
        def _():
            copy_in.wait_recv()
            work(buffer, at)

    offset = ((2 * c + core) * CLASS).astype(F32)
    turn = (4 * chip).astype(F32)

    def place_of(goal):
        if goal >= 64:
            return near_sends.at[(goal - 64) // 2, pl.ds(goal % 2 * 8, 8), :]
        return sends.at[goal // 4, pl.ds(goal % 4 * 8, 8), :]

    def pick(goals, at_core, first, fresh):
        sums = [jnp.zeros((8, RADII), F32) if fresh else place_of(goal)[...] for goal in goals]

        def step(i, sums):
            sums = list(sums)
            for z in (first + 2 * i, first + 2 * i + 1):
                numbers = gather[at_core, z, 16:18, :] - offset
                turned = jnp.where(numbers < turn, numbers + 64.0, numbers) - turn
                places = jnp.where((numbers >= 0.0) & (numbers < 64.0), turned, jnp.where(numbers < 0.0, -1.0, numbers))
                for s in range(2):
                    value = gather[at_core, z, s * 8 : s * 8 + 8, :]
                    place = jnp.broadcast_to(places[s : s + 1, :], (8, RADII))
                    for t, goal in enumerate(goals):
                        sums[t] = jnp.where(place == float(goal), value, sums[t])
            return tuple(sums)

        sums = lax.fori_loop(0, 3, step, tuple(sums))
        for goal, value in zip(goals, sums):
            place_of(goal)[...] = value

    def exchange(k, rows):
        return remote(sends.at[k, pl.ds(0, rows), :], parts.at[k, pl.ds(0, rows), :], as_.at[k], ar.at[k],
                      (p, c, (chip + k) % CHIPS * 2 + core))

    def near(i):
        return remote(near_sends.at[i], near_parts.at[chip], ns.at[i], nr.at[chip], (p, c, NEAR[i] * 2 + core))

    owns_near = early & ((y == 0) | (y == RING - 1))
    near_goal = jnp.where(y == 0, 0, LON - 1)
    near_slot = jnp.where(y == 0, 18, 26) + (x * 2 + core) * 2
    near_forward = remote(near_collected, rim.at[pl.ds(pl.multiple_of(near_slot * 8, 8), 16), :],
                          ms.at[0], mr.at[x * 2 + core], (p, c, near_goal))
    forward = remote(collected.at[pl.ds(0, 24), :], rim.at[pl.ds(pl.multiple_of(c * 24, 8), 24), :],
                     fs.at[0], fr.at[c], (p, jnp.where(upper, 0, COLAT - 1), l))
    goal_c, goal_l, goal_slot = far_side_goal(c, l)
    side_forward = remote(collected.at[pl.ds(24, 8), :], rim.at[pl.ds(pl.multiple_of(goal_slot * 8, 8), 8), :],
                          gs.at[0], gr.at[goal_slot % 8], (p, goal_c, goal_l))

    def landed(part):
        for z in range(part * 6, part * 6 + 6):
            remote(bundle(core, z), bundle(core, z), zs.at[0], zr.at[z], (p, c, l)).wait_recv()
        over(part).start()

    def shared(part):
        there = six(1 - core, part)
        remote(there, there, ts.at[0], tr.at[part], (p, c, l)).wait_recv()

    for where_, slots in ((upper, 3), (middle, 4)):
        @pl.when(where_)
        def _():
            halves = [
                (ks, [k * 4 + s for k in ks for s in range(slots)] + [64 + half * 4 + w for w in range(4)])
                for half, ks in enumerate((ORDER[:8], ORDER[8:]))
            ]
            landed(0)
            for _, goals in halves:
                pick(goals, core, 0, True)
            shared(0)
            for _, goals in halves:
                pick(goals, 1 - core, 0, False)
            landed(1)
            for _, goals in halves:
                pick(goals, core, 6, False)
            shared(1)
            for ks, goals in halves:
                pick(goals, 1 - core, 6, False)
                for k in ks:
                    if k:
                        exchange(k, slots * 8).start()
            for i in range(4):
                pl.when(chip != NEAR[i])(near(i).start)
            for k in ORDER[:-1]:
                exchange(k, slots * 8).wait_recv()
            for s in range(slots):
                total = sends[0, s * 8 : s * 8 + 8, :]
                for k in range(1, CHIPS):
                    total = total + parts[k, s * 8 : s * 8 + 8, :]
                collected[s * 8 : s * 8 + 8, :] = total

    @pl.when(middle)
    def _():
        pl.semaphore_wait(ready, 2)
        side_forward.start()

    @pl.when(early & jnp.logical_not(is_top))
    def _():
        forward.start()

    @pl.when(is_top)
    def _():
        rim[0:24, :] = collected[0:24, :]

    for i in range(4):
        @pl.when(early & (chip == NEAR[i]))
        def _():
            rest = [k for k in range(CHIPS) if k != NEAR[i]]
            for k in rest:
                remote(near_collected, near_parts.at[k], ns.at[0], nr.at[k], (p, c, l)).wait_recv()
            for s in range(2):
                total = near_sends[i, s * 8 : s * 8 + 8, :]
                for k in rest:
                    total = total + near_parts[k, s * 8 : s * 8 + 8, :]
                near_collected[s * 8 : s * 8 + 8, :] = total

    pl.when(owns_near & jnp.logical_not(is_side))(near_forward.start)
    for border, first, own in ((is_left, 18, 0), (is_right, 26, 3)):
        @pl.when(border & early)
        def _():
            rim[(first + 2 * own) * 8 : (first + 2 * own) * 8 + 16, :] = near_collected[...]
            for k in range(4):
                if k != own:
                    window = rim.at[pl.ds((first + 2 * k) * 8, 16), :]
                    remote(window, window, ms.at[0], mr.at[k], (p, c, l)).wait_recv()

        @pl.when(border & late)
        def _():
            for s in range(8):
                window = rim.at[pl.ds((first + s) * 8, 8), :]
                remote(window, window, gs.at[0], gr.at[s], (p, c, l)).wait_recv()

    for border, planes in ((is_top, (1, 2)), (is_bottom, (3, 4, 5))):
        @pl.when(border)
        def _():
            for k in planes:
                window = rim.at[pl.ds(k * 24, 24), :]
                remote(window, window, fs.at[0], fr.at[k], (p, c, l)).wait_recv()

    for border, copy_in, buffer, work, at, first, count in sides:
        @pl.when(border)
        def _():
            for n in range(8):
                buffer[n] = rim[pl.ds(first * 8 + n, count, stride=8), :]
            work(buffer, at)

    for j in range(COLS):
        for n in range(8):
            value = inc[n, j] + k_phi * (azimuth[n, j + 2] - azimuth[n, j])
            value = value + k_bottom * bottom[n, j : j + 1, :] - k_top * top[n, j : j + 1, :]
            value = jnp.where(inside, value, 0.0)
            inc[n, j] = value
            sec[n, j] = state[n, j] + 0.5 * value

    for copy in z_copies:
        copy.wait_send()

    @pl.when(early)
    def _():
        for part in range(2):
            over(part).wait_send()
        for i in range(4):
            pl.when(chip != NEAR[i])(near(i).wait_send)

    pl.when(owns_near & jnp.logical_not(is_side))(near_forward.wait_send)
    for where_, slots in ((upper, 3), (middle, 4)):
        @pl.when(where_)
        def _():
            for k in range(1, CHIPS):
                exchange(k, slots * 8).wait_send()

    pl.when(early & jnp.logical_not(is_top))(forward.wait_send)
    pl.when(middle)(side_forward.wait_send)
    pl.when(c < COLAT - 1)(to_below.wait_send)
    pl.when(c > 0)(to_above.wait_send)
    pl.when(l < LON - 1)(to_right.wait_send)
    pl.when(l > 0)(to_left.wait_send)


def write(increment, sectioned, increment_out, sectioned_out, sem):
    first = pltpu.make_async_copy(increment, increment_out, sem.at[0])
    second = pltpu.make_async_copy(sectioned, sectioned_out, sem.at[1])
    first.start()
    second.start()
    first.wait()
    second.wait()


def shards(fields, donor_cell, target_slot, donor_frac):
    hbm = pl.BlockSpec(memory_space=pl.ANY)
    vmem, dma = pltpu.VMEM, pltpu.SemaphoreType.DMA
    shape = jax.ShapeDtypeStruct((8, COLS, ROWS, RADII), F32)
    increment, sectioned = pl.pallas_call(
        kernel,
        out_shape=(pltpu.VMEM(shape.shape, F32), pltpu.VMEM(shape.shape, F32)),
        in_specs=[hbm, hbm, hbm, hbm],
        out_specs=(pl.BlockSpec(memory_space=pltpu.VMEM), pl.BlockSpec(memory_space=pltpu.VMEM)),
        scratch_shapes=[
            pltpu.SMEM(donor_cell.shape, jnp.int32),
            pltpu.SMEM(target_slot.shape, jnp.int32),
            pltpu.SMEM(donor_frac.shape, F32),
            vmem((8, COLS, ROWS, RADII), F32),
            vmem((24, RADII), F32),
            vmem((2, COLAT, 24, RADII), F32),
            vmem((CHIPS, 32, RADII), F32),
            vmem((4, 16, RADII), F32),
            vmem((CHIPS, 32, RADII), F32),
            vmem((CHIPS, 16, RADII), F32),
            vmem((32, RADII), F32),
            vmem((16, RADII), F32),
            vmem((RIM * 8, RADII), F32),
            vmem((8, COLS, RADII), F32),
            vmem((8, COLS, RADII), F32),
            vmem((8, ROWS, RADII), F32),
            vmem((8, ROWS, RADII), F32),
            vmem((4, 16, RADII), F32),
            vmem((8, COLS + 2, ROWS, RADII), F32),
            dma((4,)), dma((EARLY,)), dma((COLAT,)), dma((2,)), dma((2,)),
            dma((CHIPS,)), dma((CHIPS,)), dma((4,)), dma((CHIPS,)),
            dma((1,)), dma((EARLY,)), dma((1,)), dma((8,)), dma((1,)), dma((4,)), dma((4,)), dma((4,)),
            pltpu.SemaphoreType.REGULAR,
        ],
        compiler_params=pltpu.CompilerParams(collective_id=0, has_side_effects=True),
        cost_estimate=pl.CostEstimate(flops=30_000_000, bytes_accessed=2_000_000, transcendentals=0),
    )(jnp.transpose(fields[0], (0, 2, 1, 3)), donor_cell, target_slot, donor_frac)
    increment, sectioned = pl.pallas_call(
        write,
        out_shape=(shape, shape),
        in_specs=[pl.BlockSpec(memory_space=pltpu.VMEM)] * 2,
        out_specs=(hbm, hbm),
        scratch_shapes=[dma((2,))],
    )(pltpu.with_memory_space_constraint(increment, pltpu.VMEM), pltpu.with_memory_space_constraint(sectioned, pltpu.VMEM))
    return tuple(jnp.transpose(x, (0, 2, 1, 3))[None] for x in (increment, sectioned))


def solution(mesh):
    placed = (
        P("panel", None, "colat", "lon", None),
        P("panel", "colat", "lon"),
        P("panel", "colat", "lon"),
        P("panel", None, "colat", "lon"),
    )
    return jax.shard_map(
        shards,
        mesh=mesh,
        in_specs=placed,
        out_specs=(P("panel", None, "colat", "lon", None), P("panel", None, "colat", "lon", None)),
        check_vma=False,
    )
```

```python
import functools
import math

import jax
import jax.numpy as jnp
from jax import lax
from jax.experimental import pallas as pl
from jax.experimental.pallas import tpu as pltpu
from jax.sharding import PartitionSpec as P

GAMMA_GAS = 5.0 / 3.0
INNER_RADIUS = 0.35
MESH = pl.DeviceIdType.MESH
ROWS, COLS, RADII = 8, 9, 128
COLAT, LON, RING, CHIPS = 12, 32, 8, 16
RIM = 2 * (ROWS + COLS)
EARLY, UPPER, CLASS = 6, 3, 144
TOP = (4, 3, 2)
FIRST = (0, TOP[0], TOP[0] + TOP[1])
ORDER = (4, 12, 3, 5, 11, 13, 6, 2, 10, 14, 7, 1, 9, 15, 8, 0)
NEAR = (1, 9, 6, 14)
F32 = jnp.float32

STEP_THETA = 0.5 * math.pi / (ROWS * COLAT - 3)
STEP_PHI = 1.5 * math.pi / (COLS * LON - 3)
STEP_RADIUS = (1.0 - INNER_RADIUS) / (RADII - 1)
TIME_STEP = 0.3 * INNER_RADIUS * min(STEP_THETA, STEP_PHI)
FRAME = ((0, 1.0), (1, -1.0), (3, 1.0), (2, 1.0), (4, -1.0), (6, 1.0), (5, 1.0), (7, 1.0))


def primitives(q):
    inverse = 1.0 / q[0]
    v = [q[1] * inverse, q[2] * inverse, q[3] * inverse]
    magnet = q[4] * q[4] + q[5] * q[5] + q[6] * q[6]
    motion = q[1] * v[0] + q[2] * v[1] + q[3] * v[2]
    total = (GAMMA_GAS - 1.0) * (q[7] - 0.5 * motion - 0.5 * magnet) + 0.5 * magnet
    alignment = v[0] * q[4] + v[1] * q[5] + v[2] * q[6]
    return v, total, alignment


def flux(q, prim, d):
    v, total, alignment = prim
    vd = v[0] * d[0] + v[1] * d[1]
    bd = q[4] * d[0] + q[5] * d[1]
    if d[2] is not None:
        vd = vd + v[2] * d[2]
        bd = bd + q[6] * d[2]
    out = [q[0] * vd]
    for a in range(3):
        term = q[1 + a] * vd - q[4 + a] * bd
        if d[a] is not None:
            term = term + total * d[a]
        out.append(term)
    for a in range(3):
        out.append(vd * q[4 + a] - bd * v[a])
    out.append((q[7] + total) * vd - bd * alignment)
    return out


def owner_of(code):
    code0 = jnp.maximum(code, 0)
    device, slot = lax.div(code0, RIM), lax.rem(code0, RIM)
    c, l = lax.div(device, LON), lax.rem(device, LON)
    is_right = jnp.where(slot >= 26, 1, 0)
    w = jnp.maximum(slot - 18 - 8 * is_right, 0)
    near = c < EARLY
    v = jnp.maximum(c - EARLY, 0) * 16 + is_right * 8 + w
    is_row = slot < 18
    lon = jnp.where(is_row, l, lax.rem(v, LON))
    level = jnp.where(slot < FIRST[1], 0, jnp.where(slot < FIRST[2], 1, 2))
    base = jnp.where(slot < FIRST[1], 0, jnp.where(slot < FIRST[2], FIRST[1], FIRST[2]))
    spot = jnp.where(slot < 9, slot - base, jnp.where(is_row, lax.rem(slot, 3), 3))
    place = lax.div(lon, 2) * 8 + spot
    core = lax.rem(lon, 2)
    row_plane = jnp.where(slot < 9, level, lax.div(slot, 3))
    plane = jnp.where(is_row, row_plane, UPPER + lax.div(v, LON))
    at_side = near & jnp.logical_not(is_row)
    plane = jnp.where(at_side, c, plane)
    place = jnp.where(at_side, 128 + is_right * 4 + lax.div(w, 4) * 2 + lax.rem(w, 2), place)
    core = jnp.where(at_side, lax.rem(lax.div(w, 2), 2), core)
    return jnp.where(code < 0, -1, (plane * 2 + core) * CLASS + place)


def far_side_goal(c, l):
    v = (c - UPPER) * LON + l
    is_right = v % 16 // 8
    return EARLY + v // 16, is_right * (LON - 1), 18 + is_right * 8 + v % 8


def kernel(fields, cells_in, targets_in, frac_in, inc, sec,
           cells, targets, frac, state, mine, gather, sends, near_sends, parts, near_parts, collected, near_collected, rim, top, bottom, left, right,
           trig, azimuth, load_sem, zs, zr, ts, tr, as_, ar, ns, nr, fs, fr, gs, gr, ms, mr, hs, hr, ready):
    p, c, l = lax.axis_index("panel"), lax.axis_index("colat"), lax.axis_index("lon")
    core, x, y = l % 2, l // 16, l // 2 % RING
    chip = l // 2
    is_top, is_bottom, is_left, is_right = c == 0, c == COLAT - 1, l == 0, l == LON - 1
    early, upper = c < EARLY, c < UPPER
    middle = early & jnp.logical_not(upper)
    late = jnp.logical_not(early)
    is_side = is_left | is_right

    def remote(src, dst, send, recv, device):
        return pltpu.make_async_remote_copy(
            src_ref=src, dst_ref=dst, send_sem=send, recv_sem=recv,
            device_id=device, device_id_type=MESH)

    loads = [pltpu.make_async_copy(source, goal, load_sem.at[i])
             for i, (source, goal) in enumerate(((fields, state), (cells_in, cells), (targets_in, targets), (frac_in, frac)))]
    for load in loads:
        load.start()

    barrier = pltpu.get_barrier_semaphore()

    def greet(device):
        pl.semaphore_signal(barrier, inc=1, device_id=device, device_id_type=MESH)

    pl.when(l > 0)(lambda: greet((p, c, l - 1)))
    pl.when(l < LON - 1)(lambda: greet((p, c, l + 1)))

    pl.when(c > 0)(lambda: greet((p, c - 1, l)))
    pl.when(c < COLAT - 1)(lambda: greet((p, c + 1, l)))
    across = (1 - x) * 16 + y * 2

    @pl.when(early)
    def _():
        for k in range(COLAT):
            greet((1 - p, (c + 6 + k) % COLAT, across + core))
        for k in range(1, CHIPS):
            greet((p, c, (chip + k) % CHIPS * 2 + core))

    for border, places in ((is_left, (3, 19)), (is_right, (12, 28))):
        @pl.when(early & border)
        def _():
            for k in places:
                greet((p, c, k))

    @pl.when(middle)
    def _():
        greet((p, COLAT - 1, l))
        goal_c, goal_l, _ = far_side_goal(c, l)
        greet((p, goal_c, goal_l))

    pl.when(is_top)(lambda: greet((p, 2, l)))

    for load in loads:
        load.wait()
    for s in range(2):
        cell = cells[0, 0, s]
        i, j = lax.div(cell, COLS), lax.rem(cell, COLS)
        a, b = frac[0, 0, 0, s], frac[0, 1, 0, s]
        weights = ((1.0 - a) * (1.0 - b), a * (1.0 - b), (1.0 - a) * b, a * b)
        values = []
        for q in range(8):
            corners = (state[q, j, pl.ds(i, 1), :], state[q, j, pl.ds(i + 1, 1), :],
                       state[q, j + 1, pl.ds(i, 1), :], state[q, j + 1, pl.ds(i + 1, 1), :])
            value = weights[0] * corners[0]
            for w in range(1, 4):
                value = value + weights[w] * corners[w]
            values.append(value)
        for place, (q, sign) in enumerate(FRAME):
            mine[s * 8 + place : s * 8 + place + 1, :] = values[q] if sign > 0 else -values[q]
        mine[16 + s : 17 + s, :] = jnp.full((1, RADII), owner_of(targets[0, 0, s]).astype(F32), F32)

    pl.semaphore_wait(
        barrier,
        EARLY
        + jnp.where(is_top | is_bottom, 1, 2)
        + jnp.where(is_side, 1, 2)
        + jnp.where(early, CHIPS - 1, 0)
        + jnp.where(early & ((l == 3) | (l == 19) | (l == 12) | (l == 28)), 1, 0)
        + jnp.where(c == 2, 1, 0)
        + jnp.where(is_bottom, EARLY - UPPER, 0)
        + jnp.where(late & is_side, 8, 0),
    )

    def bundle(at_group, z):
        return gather.at[at_group, z, pl.ds(0, 18), :]

    turned_c = (c + 1) % COLAT
    z_copies = [
        remote(mine.at[pl.ds(0, 18), :], bundle(core, turned_c), zs.at[k], zr.at[turned_c], (1 - p, k, across + core))
        for k in range(EARLY)
    ]
    for copy in z_copies:
        copy.start()

    def six(at_core, part):
        return gather.at[at_core, pl.ds(part * 6, 6), pl.ds(0, 18), :]

    def over(part):
        return remote(six(core, part), six(core, part), ts.at[part], tr.at[part], (p, c, l + 1 - 2 * core))

    to_right = remote(state.at[:, COLS - 1], left, hs.at[2], hr.at[2], (p, c, l + 1))
    to_left = remote(state.at[:, 0], right, hs.at[3], hr.at[3], (p, c, l - 1))
    to_below = remote(state.at[:, :, ROWS - 1, :], top, hs.at[0], hr.at[0], (p, c + 1, l))
    to_above = remote(state.at[:, :, 0, :], bottom, hs.at[1], hr.at[1], (p, c - 1, l))
    pl.when(l < LON - 1)(to_right.start)
    pl.when(l > 0)(to_left.start)
    pl.when(c < COLAT - 1)(to_below.start)
    pl.when(c > 0)(to_above.start)

    def announce(device):
        pl.semaphore_signal(ready, inc=1, device_id=device, device_id_type=MESH)

    @pl.when(is_bottom)
    def _():
        for k in range(UPPER, EARLY):
            announce((p, k, l))

    @pl.when(late & is_side)
    def _():
        for k in range(8):
            v = (c - EARLY) * 16 + jnp.where(is_right, 8, 0) + k
            announce((p, UPPER + v // LON, v % LON))

    index = lax.broadcasted_iota(jnp.int32, (16, RADII), 0)
    theta = 0.25 * math.pi + ((c * ROWS - 1 + index).astype(F32) - 1.0) * STEP_THETA
    phi = -0.75 * math.pi + ((l * COLS - 1 + index).astype(F32) - 1.0) * STEP_PHI
    trig[0] = jnp.sin(theta)
    trig[1] = jnp.cos(theta)
    trig[2] = jnp.sin(phi)
    trig[3] = jnp.cos(phi)
    lane = lax.broadcasted_iota(jnp.int32, (ROWS, RADII), 1)
    row = lax.broadcasted_iota(jnp.int32, (ROWS, RADII), 0)
    radius = INNER_RADIUS + lane.astype(F32) * STEP_RADIUS
    square = radius * radius
    st, ct = trig[0, 1 : 1 + ROWS, :], trig[1, 1 : 1 + ROWS, :]
    angular = -TIME_STEP / (radius * st)
    k_theta = angular * (1.0 / (2.0 * STEP_THETA))
    k_phi = angular * (1.0 / (2.0 * STEP_PHI))
    k_radius = -TIME_STEP / (2.0 * STEP_RADIUS) / square
    k_below = jnp.where(row == ROWS - 1, 0.0, k_theta)
    k_above = jnp.where(row == 0, 0.0, k_theta)
    k_bottom = jnp.where(row == ROWS - 1, k_theta, 0.0)
    k_top = jnp.where(row == 0, k_theta, 0.0)
    inside = (lane > 0) & (lane < RADII - 1)

    def column(j, carry):
        q = [state[n, j] for n in range(8)]
        sp, cp = trig[2, pl.ds(j + 1, 1), :], trig[3, pl.ds(j + 1, 1), :]
        prim = primitives(q)
        f_r = flux(q, prim, (st * cp, st * sp, ct))
        f_t = flux(q, prim, (ct * cp, ct * sp, -st))
        f_p = flux(q, prim, (-sp, cp, None))
        for n in range(8):
            weighted = square * f_r[n]
            value = k_radius * (pltpu.roll(weighted, RADII - 1, 1) - pltpu.roll(weighted, 1, 1))
            slanted = st * f_t[n]
            value = value + k_below * pltpu.roll(slanted, ROWS - 1, 0) - k_above * pltpu.roll(slanted, 1, 0)
            inc[n, j] = value
            azimuth[n, j + 1] = f_p[n]
        return carry

    lax.fori_loop(0, COLS, column, 0)

    def row_edge(buffer, at):
        q = [buffer[n] for n in range(8)]
        sp, cp = trig[2, 1 : 1 + COLS, :], trig[3, 1 : 1 + COLS, :]
        edge_st, edge_ct = trig[0, at : at + 1, :], trig[1, at : at + 1, :]
        f_t = flux(q, primitives(q), (edge_ct * cp, edge_ct * sp, -edge_st))
        for n in range(8):
            buffer[n] = edge_st * f_t[n]

    def column_edge(buffer, at):
        q = [buffer[n] for n in range(8)]
        f_p = flux(q, primitives(q), (-trig[2, at : at + 1, :], trig[3, at : at + 1, :], None))
        for n in range(8):
            azimuth[n, at] = f_p[n]

    sides = (
        (is_top, to_below, top, row_edge, 0, 0, 9),
        (is_bottom, to_above, bottom, row_edge, ROWS + 1, 9, 9),
        (is_left, to_right, left, column_edge, 0, 18, 8),
        (is_right, to_left, right, column_edge, COLS + 1, 26, 8),
    )
    for border, copy_in, buffer, work, at, first, count in sides:
        @pl.when(jnp.logical_not(border))
        def _():
            copy_in.wait_recv()
            work(buffer, at)

    offset = ((2 * c + core) * CLASS).astype(F32)
    turn = (8 * chip).astype(F32)

    def place_of(goal):
        if goal >= 128:
            return near_sends.at[(goal - 128) // 2, pl.ds(goal % 2 * 8, 8), :]
        return sends.at[goal // 8, pl.ds(goal % 8 * 8, 8), :]

    def pick(goals, at_core, first, fresh):
        sums = [jnp.zeros((8, RADII), F32) if fresh else place_of(goal)[...] for goal in goals]

        def step(i, sums):
            sums = list(sums)
            for z in (first + 2 * i, first + 2 * i + 1):
                numbers = gather[at_core, z, 16:18, :] - offset
                turned = jnp.where(numbers < turn, numbers + 128.0, numbers) - turn
                places = jnp.where((numbers >= 0.0) & (numbers < 128.0), turned, jnp.where(numbers < 0.0, -1.0, numbers))
                for s in range(2):
                    value = gather[at_core, z, s * 8 : s * 8 + 8, :]
                    place = jnp.broadcast_to(places[s : s + 1, :], (8, RADII))
                    for t, goal in enumerate(goals):
                        sums[t] = jnp.where(place == float(goal), value, sums[t])
            return tuple(sums)

        sums = lax.fori_loop(0, 3, step, tuple(sums))
        for goal, value in zip(goals, sums):
            place_of(goal)[...] = value

    def exchange(k, rows):
        return remote(sends.at[k, pl.ds(0, rows), :], parts.at[k, pl.ds(0, rows), :], as_.at[k], ar.at[k],
                      (p, c, (chip + k) % CHIPS * 2 + core))

    def near(i):
        return remote(near_sends.at[i], near_parts.at[chip], ns.at[i], nr.at[chip], (p, c, NEAR[i] * 2 + core))

    owns_near = early & ((y == 1) | (y == 6))
    near_goal = jnp.where(y == 1, 0, LON - 1)
    near_slot = jnp.where(y == 1, 18, 26) + (x * 2 + core) * 2
    near_forward = remote(near_collected, rim.at[pl.ds(pl.multiple_of(near_slot * 8, 8), 16), :],
                          ms.at[0], mr.at[x * 2 + core], (p, c, near_goal))
    def to_top(level):
        rows = TOP[level] * 8
        return remote(collected.at[pl.ds(0, rows), :], rim.at[pl.ds(FIRST[level] * 8, rows), :],
                      fs.at[0], fr.at[level], (p, 0, l))

    forward = remote(collected.at[pl.ds(0, 24), :], rim.at[pl.ds(pl.multiple_of(c * 24, 8), 24), :],
                     fs.at[0], fr.at[c], (p, COLAT - 1, l))
    goal_c, goal_l, goal_slot = far_side_goal(c, l)
    side_forward = remote(collected.at[pl.ds(24, 8), :], rim.at[pl.ds(pl.multiple_of(goal_slot * 8, 8), 8), :],
                          gs.at[0], gr.at[goal_slot % 8], (p, goal_c, goal_l))

    def landed(part):
        for z in range(part * 6, part * 6 + 6):
            remote(bundle(core, z), bundle(core, z), zs.at[0], zr.at[z], (p, c, l)).wait_recv()
        over(part).start()

    def shared(part):
        there = six(1 - core, part)
        remote(there, there, ts.at[0], tr.at[part], (p, c, l)).wait_recv()

    def near_all():
        for i in range(4):
            pl.when(chip != NEAR[i])(near(i).start)

    def near_total():
        for i in range(4):
            @pl.when(chip == NEAR[i])
            def _():
                rest = [k for k in range(CHIPS) if k != NEAR[i]]
                for k in rest:
                    remote(near_collected, near_parts.at[k], ns.at[0], nr.at[k], (p, c, l)).wait_recv()
                for s in range(2):
                    total = near_sends[i, s * 8 : s * 8 + 8, :]
                    for k in rest:
                        total = total + near_parts[k, s * 8 : s * 8 + 8, :]
                    near_collected[s * 8 : s * 8 + 8, :] = total

        pl.when(owns_near)(near_forward.start)

    levels = ((is_top, TOP[0], 0), (c == 1, TOP[1], 1), (c == 2, TOP[2], 2), (middle, 4, 3))
    for where_, slots, level in levels:
        @pl.when(where_)
        def _():
            sides_first = level in (0, 3)
            count = 2 if slots > 2 else 1
            chunks = []
            for i in range(count if slots else 0):
                ks = ORDER[16 // count * i : 16 // count * (i + 1)]
                chunks.append((ks, [k * 8 + s for k in ks for s in range(slots)]))
            sides_chunk = ((), [128 + w for w in range(8)])
            chunks.insert((0, 1, len(chunks), 0)[level], sides_chunk)
            landed(0)
            for _, goals in chunks:
                pick(goals, core, 0, True)
            shared(0)
            for _, goals in chunks:
                pick(goals, 1 - core, 0, False)
            landed(1)
            for _, goals in chunks:
                pick(goals, core, 6, False)
            shared(1)
            for ks, goals in chunks:
                pick(goals, 1 - core, 6, False)
                for k in ks:
                    if k:
                        exchange(k, slots * 8).start()
                if not ks:
                    near_all()
            if sides_first:
                near_total()
            if slots:
                for k in ORDER[:-1]:
                    exchange(k, slots * 8).wait_recv()
            for s in range(slots):
                total = sends[0, s * 8 : s * 8 + 8, :]
                for k in range(1, CHIPS):
                    total = total + parts[k, s * 8 : s * 8 + 8, :]
                collected[s * 8 : s * 8 + 8, :] = total
            if level in (1, 2):
                to_top(level).start()
            if level == 0:
                rim[0 : slots * 8, :] = collected[0 : slots * 8, :]
            if not sides_first:
                near_total()

    @pl.when(middle)
    def _():
        pl.semaphore_wait(ready, 2)
        side_forward.start()
        forward.start()

    for border, first in ((is_left, 18), (is_right, 26)):
        @pl.when(border & early)
        def _():
            for k in range(4):
                window = rim.at[pl.ds((first + 2 * k) * 8, 16), :]
                remote(window, window, ms.at[0], mr.at[k], (p, c, l)).wait_recv()

        @pl.when(border & late)
        def _():
            for s in range(8):
                window = rim.at[pl.ds((first + s) * 8, 8), :]
                remote(window, window, gs.at[0], gr.at[s], (p, c, l)).wait_recv()

    pl.when(is_top)(to_top(1).wait_recv)
    pl.when(is_top)(to_top(2).wait_recv)
    for border, planes in ((is_bottom, (3, 4, 5)),):
        @pl.when(border)
        def _():
            for k in planes:
                window = rim.at[pl.ds(k * 24, 24), :]
                remote(window, window, fs.at[0], fr.at[k], (p, c, l)).wait_recv()

    for border, copy_in, buffer, work, at, first, count in sides:
        @pl.when(border)
        def _():
            for n in range(8):
                buffer[n] = rim[pl.ds(first * 8 + n, count, stride=8), :]
            work(buffer, at)

    for j in range(COLS):
        for n in range(8):
            value = inc[n, j] + k_phi * (azimuth[n, j + 2] - azimuth[n, j])
            value = value + k_bottom * bottom[n, j : j + 1, :] - k_top * top[n, j : j + 1, :]
            value = jnp.where(inside, value, 0.0)
            inc[n, j] = value
            sec[n, j] = state[n, j] + 0.5 * value

    for copy in z_copies:
        copy.wait_send()

    @pl.when(early)
    def _():
        for part in range(2):
            over(part).wait_send()
        for i in range(4):
            pl.when(chip != NEAR[i])(near(i).wait_send)

    pl.when(owns_near)(near_forward.wait_send)
    for where_, slots, level in levels:
        @pl.when(where_)
        def _():
            for k in range(1, CHIPS if slots else 1):
                exchange(k, slots * 8).wait_send()

    pl.when(c == 1)(to_top(1).wait_send)
    pl.when(c == 2)(to_top(2).wait_send)
    pl.when(middle)(forward.wait_send)
    pl.when(middle)(side_forward.wait_send)
    pl.when(c < COLAT - 1)(to_below.wait_send)
    pl.when(c > 0)(to_above.wait_send)
    pl.when(l < LON - 1)(to_right.wait_send)
    pl.when(l > 0)(to_left.wait_send)


def write(increment, sectioned, increment_out, sectioned_out, sem):
    first = pltpu.make_async_copy(increment, increment_out, sem.at[0])
    second = pltpu.make_async_copy(sectioned, sectioned_out, sem.at[1])
    first.start()
    second.start()
    first.wait()
    second.wait()


def shards(fields, donor_cell, target_slot, donor_frac):
    hbm = pl.BlockSpec(memory_space=pl.ANY)
    vmem, dma = pltpu.VMEM, pltpu.SemaphoreType.DMA
    shape = jax.ShapeDtypeStruct((8, COLS, ROWS, RADII), F32)
    increment, sectioned = pl.pallas_call(
        kernel,
        out_shape=(pltpu.VMEM(shape.shape, F32), pltpu.VMEM(shape.shape, F32)),
        in_specs=[hbm, hbm, hbm, hbm],
        out_specs=(pl.BlockSpec(memory_space=pltpu.VMEM), pl.BlockSpec(memory_space=pltpu.VMEM)),
        scratch_shapes=[
            pltpu.SMEM(donor_cell.shape, jnp.int32),
            pltpu.SMEM(target_slot.shape, jnp.int32),
            pltpu.SMEM(donor_frac.shape, F32),
            vmem((8, COLS, ROWS, RADII), F32),
            vmem((24, RADII), F32),
            vmem((2, COLAT, 24, RADII), F32),
            vmem((CHIPS, 56, RADII), F32),
            vmem((4, 16, RADII), F32),
            vmem((CHIPS, 56, RADII), F32),
            vmem((CHIPS, 16, RADII), F32),
            vmem((56, RADII), F32),
            vmem((16, RADII), F32),
            vmem((RIM * 8, RADII), F32),
            vmem((8, COLS, RADII), F32),
            vmem((8, COLS, RADII), F32),
            vmem((8, ROWS, RADII), F32),
            vmem((8, ROWS, RADII), F32),
            vmem((4, 16, RADII), F32),
            vmem((8, COLS + 2, ROWS, RADII), F32),
            dma((4,)), dma((EARLY,)), dma((COLAT,)), dma((2,)), dma((2,)),
            dma((CHIPS,)), dma((CHIPS,)), dma((4,)), dma((CHIPS,)),
            dma((1,)), dma((EARLY,)), dma((1,)), dma((8,)), dma((1,)), dma((4,)), dma((4,)), dma((4,)),
            pltpu.SemaphoreType.REGULAR,
        ],
        compiler_params=pltpu.CompilerParams(collective_id=0, has_side_effects=True),
        cost_estimate=pl.CostEstimate(flops=30_000_000, bytes_accessed=2_000_000, transcendentals=0),
    )(jnp.transpose(fields[0], (0, 2, 1, 3)), donor_cell, target_slot, donor_frac)
    increment, sectioned = pl.pallas_call(
        write,
        out_shape=(shape, shape),
        in_specs=[pl.BlockSpec(memory_space=pltpu.VMEM)] * 2,
        out_specs=(hbm, hbm),
        scratch_shapes=[dma((2,))],
    )(pltpu.with_memory_space_constraint(increment, pltpu.VMEM), pltpu.with_memory_space_constraint(sectioned, pltpu.VMEM))
    return tuple(jnp.transpose(x, (0, 2, 1, 3))[None] for x in (increment, sectioned))


def solution(mesh):
    placed = (
        P("panel", None, "colat", "lon", None),
        P("panel", "colat", "lon"),
        P("panel", "colat", "lon"),
        P("panel", None, "colat", "lon"),
    )
    return jax.shard_map(
        shards,
        mesh=mesh,
        in_specs=placed,
        out_specs=(P("panel", None, "colat", "lon", None), P("panel", None, "colat", "lon", None)),
        check_vma=False,
    )
```

```python
import functools
import math

import jax
import jax.numpy as jnp
from jax import lax
from jax.experimental import pallas as pl
from jax.experimental.pallas import tpu as pltpu
from jax.sharding import PartitionSpec as P

GAMMA_GAS = 5.0 / 3.0
INNER_RADIUS = 0.35
MESH = pl.DeviceIdType.MESH
ROWS, COLS, RADII = 8, 9, 128
COLAT, LON, RING, CHIPS = 12, 32, 8, 16
RIM = 2 * (ROWS + COLS)
EARLY, UPPER, CLASS = 6, 3, 144
TOP = (4, 3, 2)
FIRST = (0, TOP[0], TOP[0] + TOP[1])
ORDER = (4, 12, 3, 5, 11, 13, 6, 2, 10, 14, 7, 1, 9, 15, 8, 0)
NEAR = (1, 9, 6, 14)
F32 = jnp.float32

STEP_THETA = 0.5 * math.pi / (ROWS * COLAT - 3)
STEP_PHI = 1.5 * math.pi / (COLS * LON - 3)
STEP_RADIUS = (1.0 - INNER_RADIUS) / (RADII - 1)
TIME_STEP = 0.3 * INNER_RADIUS * min(STEP_THETA, STEP_PHI)
FRAME = ((0, 1.0), (1, -1.0), (3, 1.0), (2, 1.0), (4, -1.0), (6, 1.0), (5, 1.0), (7, 1.0))


def primitives(q):
    inverse = 1.0 / q[0]
    v = [q[1] * inverse, q[2] * inverse, q[3] * inverse]
    magnet = q[4] * q[4] + q[5] * q[5] + q[6] * q[6]
    motion = q[1] * v[0] + q[2] * v[1] + q[3] * v[2]
    total = (GAMMA_GAS - 1.0) * (q[7] - 0.5 * motion - 0.5 * magnet) + 0.5 * magnet
    alignment = v[0] * q[4] + v[1] * q[5] + v[2] * q[6]
    return v, total, alignment


def flux(q, prim, d):
    v, total, alignment = prim
    vd = v[0] * d[0] + v[1] * d[1]
    bd = q[4] * d[0] + q[5] * d[1]
    if d[2] is not None:
        vd = vd + v[2] * d[2]
        bd = bd + q[6] * d[2]
    out = [q[0] * vd]
    for a in range(3):
        term = q[1 + a] * vd - q[4 + a] * bd
        if d[a] is not None:
            term = term + total * d[a]
        out.append(term)
    for a in range(3):
        out.append(vd * q[4 + a] - bd * v[a])
    out.append((q[7] + total) * vd - bd * alignment)
    return out


def owner_of(code):
    code0 = jnp.maximum(code, 0)
    device, slot = lax.div(code0, RIM), lax.rem(code0, RIM)
    c, l = lax.div(device, LON), lax.rem(device, LON)
    is_right = jnp.where(slot >= 26, 1, 0)
    w = jnp.maximum(slot - 18 - 8 * is_right, 0)
    near = c < EARLY
    v = jnp.maximum(c - EARLY, 0) * 16 + is_right * 8 + w
    is_row = slot < 18
    lon = jnp.where(is_row, l, lax.rem(v, LON))
    level = jnp.where(slot < FIRST[1], 0, jnp.where(slot < FIRST[2], 1, 2))
    base = jnp.where(slot < FIRST[1], 0, jnp.where(slot < FIRST[2], FIRST[1], FIRST[2]))
    spot = jnp.where(slot < 9, slot - base, jnp.where(is_row, lax.rem(slot, 3), 3))
    place = lax.div(lon, 2) * 8 + spot
    core = lax.rem(lon, 2)
    row_plane = jnp.where(slot < 9, level, lax.div(slot, 3))
    plane = jnp.where(is_row, row_plane, UPPER + lax.div(v, LON))
    at_side = near & jnp.logical_not(is_row)
    plane = jnp.where(at_side, c, plane)
    place = jnp.where(at_side, 128 + is_right * 4 + lax.div(w, 4) * 2 + lax.rem(w, 2), place)
    core = jnp.where(at_side, lax.rem(lax.div(w, 2), 2), core)
    return jnp.where(code < 0, -1, (plane * 2 + core) * CLASS + place)


def far_side_goal(c, l):
    v = (c - UPPER) * LON + l
    is_right = v % 16 // 8
    return EARLY + v // 16, is_right * (LON - 1), 18 + is_right * 8 + v % 8


def kernel(fields, cells_in, targets_in, frac_in, inc, sec,
           cells, targets, frac, state, mine, gather, sends, near_sends, parts, near_parts, collected, near_collected, rim, top, bottom, left, right,
           trig, azimuth, load_sem, zs, zr, ts, tr, as_, ar, ns, nr, fs, fr, gs, gr, ms, mr, hs, hr, ready):
    p, c, l = lax.axis_index("panel"), lax.axis_index("colat"), lax.axis_index("lon")
    core, x, y = l % 2, l // 16, l // 2 % RING
    chip = l // 2
    is_top, is_bottom, is_left, is_right = c == 0, c == COLAT - 1, l == 0, l == LON - 1
    early, upper = c < EARLY, c < UPPER
    middle = early & jnp.logical_not(upper)
    late = jnp.logical_not(early)
    is_side = is_left | is_right

    def remote(src, dst, send, recv, device):
        return pltpu.make_async_remote_copy(
            src_ref=src, dst_ref=dst, send_sem=send, recv_sem=recv,
            device_id=device, device_id_type=MESH)

    loads = [pltpu.make_async_copy(source, goal, load_sem.at[i])
             for i, (source, goal) in enumerate(((fields, state), (cells_in, cells), (targets_in, targets), (frac_in, frac)))]
    for load in loads:
        load.start()

    barrier = pltpu.get_barrier_semaphore()

    def greet(device):
        pl.semaphore_signal(barrier, inc=1, device_id=device, device_id_type=MESH)

    pl.when(l > 0)(lambda: greet((p, c, l - 1)))
    pl.when(l < LON - 1)(lambda: greet((p, c, l + 1)))

    pl.when(c > 0)(lambda: greet((p, c - 1, l)))
    pl.when(c < COLAT - 1)(lambda: greet((p, c + 1, l)))
    across = (1 - x) * 16 + y * 2

    @pl.when(early)
    def _():
        for k in range(COLAT):
            greet((1 - p, (c + 6 + k) % COLAT, across + 1 - core))
        for k in range(1, CHIPS):
            greet((p, c, (chip + k) % CHIPS * 2 + core))

    for border, places in ((is_left, (3, 19)), (is_right, (12, 28))):
        @pl.when(early & border)
        def _():
            for k in places:
                greet((p, c, k))

    @pl.when(middle)
    def _():
        greet((p, COLAT - 1, l))
        goal_c, goal_l, _ = far_side_goal(c, l)
        greet((p, goal_c, goal_l))

    pl.when(is_top)(lambda: greet((p, 2, l)))

    for load in loads:
        load.wait()
    for s in range(2):
        cell = cells[0, 0, s]
        i, j = lax.div(cell, COLS), lax.rem(cell, COLS)
        a, b = frac[0, 0, 0, s], frac[0, 1, 0, s]
        weights = ((1.0 - a) * (1.0 - b), a * (1.0 - b), (1.0 - a) * b, a * b)
        values = []
        for q in range(8):
            corners = (state[q, j, pl.ds(i, 1), :], state[q, j, pl.ds(i + 1, 1), :],
                       state[q, j + 1, pl.ds(i, 1), :], state[q, j + 1, pl.ds(i + 1, 1), :])
            value = weights[0] * corners[0]
            for w in range(1, 4):
                value = value + weights[w] * corners[w]
            values.append(value)
        for place, (q, sign) in enumerate(FRAME):
            mine[s * 8 + place : s * 8 + place + 1, :] = values[q] if sign > 0 else -values[q]
        mine[16 + s : 17 + s, :] = jnp.full((1, RADII), owner_of(targets[0, 0, s]).astype(F32), F32)

    pl.semaphore_wait(
        barrier,
        EARLY
        + jnp.where(is_top | is_bottom, 1, 2)
        + jnp.where(is_side, 1, 2)
        + jnp.where(early, CHIPS - 1, 0)
        + jnp.where(early & ((l == 3) | (l == 19) | (l == 12) | (l == 28)), 1, 0)
        + jnp.where(c == 2, 1, 0)
        + jnp.where(is_bottom, EARLY - UPPER, 0)
        + jnp.where(late & is_side, 8, 0),
    )

    def bundle(at_group, z):
        return gather.at[at_group, z, pl.ds(0, 18), :]

    turned_c = (c + 1) % COLAT
    z_copies = [
        remote(mine.at[pl.ds(0, 18), :], bundle(1 - core, turned_c), zs.at[k], zr.at[turned_c], (1 - p, k, across + 1 - core))
        for k in range(EARLY)
    ]
    for k in (2, 1, 0, 3, 4, 5):
        z_copies[k].start()

    def six(at_core, part):
        return gather.at[at_core, pl.ds(part * 6, 6), pl.ds(0, 18), :]

    def over(part):
        return remote(six(core, part), six(core, part), ts.at[part], tr.at[part], (p, c, l + 1 - 2 * core))

    to_right = remote(state.at[:, COLS - 1], left, hs.at[2], hr.at[2], (p, c, l + 1))
    to_left = remote(state.at[:, 0], right, hs.at[3], hr.at[3], (p, c, l - 1))
    to_below = remote(state.at[:, :, ROWS - 1, :], top, hs.at[0], hr.at[0], (p, c + 1, l))
    to_above = remote(state.at[:, :, 0, :], bottom, hs.at[1], hr.at[1], (p, c - 1, l))
    pl.when(l < LON - 1)(to_right.start)
    pl.when(l > 0)(to_left.start)
    pl.when(c < COLAT - 1)(to_below.start)
    pl.when(c > 0)(to_above.start)

    def announce(device):
        pl.semaphore_signal(ready, inc=1, device_id=device, device_id_type=MESH)

    @pl.when(is_bottom)
    def _():
        for k in range(UPPER, EARLY):
            announce((p, k, l))

    @pl.when(late & is_side)
    def _():
        for k in range(8):
            v = (c - EARLY) * 16 + jnp.where(is_right, 8, 0) + k
            announce((p, UPPER + v // LON, v % LON))

    index = lax.broadcasted_iota(jnp.int32, (16, RADII), 0)
    theta = 0.25 * math.pi + ((c * ROWS - 1 + index).astype(F32) - 1.0) * STEP_THETA
    phi = -0.75 * math.pi + ((l * COLS - 1 + index).astype(F32) - 1.0) * STEP_PHI
    trig[0] = jnp.sin(theta)
    trig[1] = jnp.cos(theta)
    trig[2] = jnp.sin(phi)
    trig[3] = jnp.cos(phi)
    lane = lax.broadcasted_iota(jnp.int32, (ROWS, RADII), 1)
    row = lax.broadcasted_iota(jnp.int32, (ROWS, RADII), 0)
    radius = INNER_RADIUS + lane.astype(F32) * STEP_RADIUS
    square = radius * radius
    st, ct = trig[0, 1 : 1 + ROWS, :], trig[1, 1 : 1 + ROWS, :]
    angular = -TIME_STEP / (radius * st)
    k_theta = angular * (1.0 / (2.0 * STEP_THETA))
    k_phi = angular * (1.0 / (2.0 * STEP_PHI))
    k_radius = -TIME_STEP / (2.0 * STEP_RADIUS) / square
    k_below = jnp.where(row == ROWS - 1, 0.0, k_theta)
    k_above = jnp.where(row == 0, 0.0, k_theta)
    k_bottom = jnp.where(row == ROWS - 1, k_theta, 0.0)
    k_top = jnp.where(row == 0, k_theta, 0.0)
    inside = (lane > 0) & (lane < RADII - 1)

    def column(j, carry):
        q = [state[n, j] for n in range(8)]
        sp, cp = trig[2, pl.ds(j + 1, 1), :], trig[3, pl.ds(j + 1, 1), :]
        prim = primitives(q)
        f_r = flux(q, prim, (st * cp, st * sp, ct))
        f_t = flux(q, prim, (ct * cp, ct * sp, -st))
        f_p = flux(q, prim, (-sp, cp, None))
        for n in range(8):
            weighted = square * f_r[n]
            value = k_radius * (pltpu.roll(weighted, RADII - 1, 1) - pltpu.roll(weighted, 1, 1))
            slanted = st * f_t[n]
            value = value + k_below * pltpu.roll(slanted, ROWS - 1, 0) - k_above * pltpu.roll(slanted, 1, 0)
            inc[n, j] = value
            azimuth[n, j + 1] = f_p[n]
        return carry

    lax.fori_loop(0, COLS, column, 0)

    def row_edge(buffer, at):
        q = [buffer[n] for n in range(8)]
        sp, cp = trig[2, 1 : 1 + COLS, :], trig[3, 1 : 1 + COLS, :]
        edge_st, edge_ct = trig[0, at : at + 1, :], trig[1, at : at + 1, :]
        f_t = flux(q, primitives(q), (edge_ct * cp, edge_ct * sp, -edge_st))
        for n in range(8):
            buffer[n] = edge_st * f_t[n]

    def column_edge(buffer, at):
        q = [buffer[n] for n in range(8)]
        f_p = flux(q, primitives(q), (-trig[2, at : at + 1, :], trig[3, at : at + 1, :], None))
        for n in range(8):
            azimuth[n, at] = f_p[n]

    sides = (
        (is_top, to_below, top, row_edge, 0, 0, 9),
        (is_bottom, to_above, bottom, row_edge, ROWS + 1, 9, 9),
        (is_left, to_right, left, column_edge, 0, 18, 8),
        (is_right, to_left, right, column_edge, COLS + 1, 26, 8),
    )
    for border, copy_in, buffer, work, at, first, count in sides:
        @pl.when(jnp.logical_not(border))
        def _():
            copy_in.wait_recv()
            work(buffer, at)

    offset = ((2 * c + core) * CLASS).astype(F32)
    turn = (8 * chip).astype(F32)

    def place_of(goal):
        if goal >= 128:
            return near_sends.at[(goal - 128) // 2, pl.ds(goal % 2 * 8, 8), :]
        return sends.at[goal // 8, pl.ds(goal % 8 * 8, 8), :]

    def pick(goals, at_core, first, fresh):
        sums = [jnp.zeros((8, RADII), F32) if fresh else place_of(goal)[...] for goal in goals]

        def step(i, sums):
            sums = list(sums)
            for z in (first + 2 * i, first + 2 * i + 1):
                numbers = gather[at_core, z, 16:18, :] - offset
                turned = jnp.where(numbers < turn, numbers + 128.0, numbers) - turn
                places = jnp.where((numbers >= 0.0) & (numbers < 128.0), turned, jnp.where(numbers < 0.0, -1.0, numbers))
                for s in range(2):
                    value = gather[at_core, z, s * 8 : s * 8 + 8, :]
                    place = jnp.broadcast_to(places[s : s + 1, :], (8, RADII))
                    for t, goal in enumerate(goals):
                        sums[t] = jnp.where(place == float(goal), value, sums[t])
            return tuple(sums)

        sums = lax.fori_loop(0, 3, step, tuple(sums), unroll=3)
        for goal, value in zip(goals, sums):
            place_of(goal)[...] = value

    def exchange(k, rows):
        return remote(sends.at[k, pl.ds(0, rows), :], parts.at[k, pl.ds(0, rows), :], as_.at[k], ar.at[k],
                      (p, c, (chip + k) % CHIPS * 2 + core))

    def near(i):
        return remote(near_sends.at[i], near_parts.at[chip], ns.at[i], nr.at[chip], (p, c, NEAR[i] * 2 + core))

    owns_near = early & ((y == 1) | (y == 6))
    near_goal = jnp.where(y == 1, 0, LON - 1)
    near_slot = jnp.where(y == 1, 18, 26) + (x * 2 + core) * 2
    near_forward = remote(near_collected, rim.at[pl.ds(pl.multiple_of(near_slot * 8, 8), 16), :],
                          ms.at[0], mr.at[x * 2 + core], (p, c, near_goal))
    def to_top(level):
        rows = TOP[level] * 8
        return remote(collected.at[pl.ds(0, rows), :], rim.at[pl.ds(FIRST[level] * 8, rows), :],
                      fs.at[0], fr.at[level], (p, 0, l))

    forward = remote(collected.at[pl.ds(0, 24), :], rim.at[pl.ds(pl.multiple_of(c * 24, 8), 24), :],
                     fs.at[0], fr.at[c], (p, COLAT - 1, l))
    goal_c, goal_l, goal_slot = far_side_goal(c, l)
    side_forward = remote(collected.at[pl.ds(24, 8), :], rim.at[pl.ds(pl.multiple_of(goal_slot * 8, 8), 8), :],
                          gs.at[0], gr.at[goal_slot % 8], (p, goal_c, goal_l))

    def landed(part):
        for z in range(part * 6, part * 6 + 6):
            remote(bundle(core, z), bundle(core, z), zs.at[0], zr.at[z], (p, c, l)).wait_recv()
        over(part).start()

    def shared(part):
        there = six(1 - core, part)
        remote(there, there, ts.at[0], tr.at[part], (p, c, l)).wait_recv()

    def near_all():
        for i in range(4):
            pl.when(chip != NEAR[i])(near(i).start)

    def near_total():
        for i in range(4):
            @pl.when(chip == NEAR[i])
            def _():
                rest = [k for k in range(CHIPS) if k != NEAR[i]]
                for k in rest:
                    remote(near_collected, near_parts.at[k], ns.at[0], nr.at[k], (p, c, l)).wait_recv()
                for s in range(2):
                    total = near_sends[i, s * 8 : s * 8 + 8, :]
                    for k in rest:
                        total = total + near_parts[k, s * 8 : s * 8 + 8, :]
                    near_collected[s * 8 : s * 8 + 8, :] = total

        pl.when(owns_near)(near_forward.start)

    levels = ((is_top, TOP[0], 0), (c == 1, TOP[1], 1), (c == 2, TOP[2], 2), (middle, 4, 3))
    for where_, slots, level in levels:
        @pl.when(where_)
        def _():
            sides_first = level in (0, 3)
            count = 2 if slots > 2 else 1
            chunks = []
            for i in range(count if slots else 0):
                ks = ORDER[16 // count * i : 16 // count * (i + 1)]
                chunks.append((ks, [k * 8 + s for k in ks for s in range(slots)]))
            sides_chunk = ((), [128 + w for w in range(8)])
            chunks.insert((0, 1, len(chunks), 0)[level], sides_chunk)
            landed(0)
            for _, goals in chunks:
                pick(goals, core, 0, True)
            shared(0)
            for _, goals in chunks:
                pick(goals, 1 - core, 0, False)
            landed(1)
            for _, goals in chunks:
                pick(goals, core, 6, False)
            shared(1)
            for ks, goals in chunks:
                pick(goals, 1 - core, 6, False)
                for k in ks:
                    if k:
                        exchange(k, slots * 8).start()
                if not ks:
                    near_all()
            if sides_first:
                near_total()
            if slots:
                for k in ORDER[:-1]:
                    exchange(k, slots * 8).wait_recv()
            for s in range(slots):
                total = sends[0, s * 8 : s * 8 + 8, :]
                for k in range(1, CHIPS):
                    total = total + parts[k, s * 8 : s * 8 + 8, :]
                collected[s * 8 : s * 8 + 8, :] = total
            if level in (1, 2):
                to_top(level).start()
            if level == 0:
                rim[0 : slots * 8, :] = collected[0 : slots * 8, :]
            if not sides_first:
                near_total()

    @pl.when(middle)
    def _():
        pl.semaphore_wait(ready, 2)
        side_forward.start()
        forward.start()

    for border, first in ((is_left, 18), (is_right, 26)):
        @pl.when(border & early)
        def _():
            for k in range(4):
                window = rim.at[pl.ds((first + 2 * k) * 8, 16), :]
                remote(window, window, ms.at[0], mr.at[k], (p, c, l)).wait_recv()

        @pl.when(border & late)
        def _():
            for s in range(8):
                window = rim.at[pl.ds((first + s) * 8, 8), :]
                remote(window, window, gs.at[0], gr.at[s], (p, c, l)).wait_recv()

    pl.when(is_top)(to_top(1).wait_recv)
    pl.when(is_top)(to_top(2).wait_recv)
    for border, planes in ((is_bottom, (3, 4, 5)),):
        @pl.when(border)
        def _():
            for k in planes:
                window = rim.at[pl.ds(k * 24, 24), :]
                remote(window, window, fs.at[0], fr.at[k], (p, c, l)).wait_recv()

    for border, copy_in, buffer, work, at, first, count in sides:
        @pl.when(border)
        def _():
            for n in range(8):
                buffer[n] = rim[pl.ds(first * 8 + n, count, stride=8), :]
            work(buffer, at)

    for j in range(COLS):
        for n in range(8):
            value = inc[n, j] + k_phi * (azimuth[n, j + 2] - azimuth[n, j])
            value = value + k_bottom * bottom[n, j : j + 1, :] - k_top * top[n, j : j + 1, :]
            value = jnp.where(inside, value, 0.0)
            inc[n, j] = value
            sec[n, j] = state[n, j] + 0.5 * value

    for copy in z_copies:
        copy.wait_send()

    @pl.when(early)
    def _():
        for part in range(2):
            over(part).wait_send()
        for i in range(4):
            pl.when(chip != NEAR[i])(near(i).wait_send)

    pl.when(owns_near)(near_forward.wait_send)
    for where_, slots, level in levels:
        @pl.when(where_)
        def _():
            for k in range(1, CHIPS if slots else 1):
                exchange(k, slots * 8).wait_send()

    pl.when(c == 1)(to_top(1).wait_send)
    pl.when(c == 2)(to_top(2).wait_send)
    pl.when(middle)(forward.wait_send)
    pl.when(middle)(side_forward.wait_send)
    pl.when(c < COLAT - 1)(to_below.wait_send)
    pl.when(c > 0)(to_above.wait_send)
    pl.when(l < LON - 1)(to_right.wait_send)
    pl.when(l > 0)(to_left.wait_send)


def write(increment, sectioned, increment_out, sectioned_out, sem):
    first = pltpu.make_async_copy(increment, increment_out, sem.at[0])
    second = pltpu.make_async_copy(sectioned, sectioned_out, sem.at[1])
    first.start()
    second.start()
    first.wait()
    second.wait()


def shards(fields, donor_cell, target_slot, donor_frac):
    hbm = pl.BlockSpec(memory_space=pl.ANY)
    vmem, dma = pltpu.VMEM, pltpu.SemaphoreType.DMA
    shape = jax.ShapeDtypeStruct((8, COLS, ROWS, RADII), F32)
    increment, sectioned = pl.pallas_call(
        kernel,
        out_shape=(pltpu.VMEM(shape.shape, F32), pltpu.VMEM(shape.shape, F32)),
        in_specs=[hbm, hbm, hbm, hbm],
        out_specs=(pl.BlockSpec(memory_space=pltpu.VMEM), pl.BlockSpec(memory_space=pltpu.VMEM)),
        scratch_shapes=[
            pltpu.SMEM(donor_cell.shape, jnp.int32),
            pltpu.SMEM(target_slot.shape, jnp.int32),
            pltpu.SMEM(donor_frac.shape, F32),
            vmem((8, COLS, ROWS, RADII), F32),
            vmem((24, RADII), F32),
            vmem((2, COLAT, 24, RADII), F32),
            vmem((CHIPS, 56, RADII), F32),
            vmem((4, 16, RADII), F32),
            vmem((CHIPS, 56, RADII), F32),
            vmem((CHIPS, 16, RADII), F32),
            vmem((56, RADII), F32),
            vmem((16, RADII), F32),
            vmem((RIM * 8, RADII), F32),
            vmem((8, COLS, RADII), F32),
            vmem((8, COLS, RADII), F32),
            vmem((8, ROWS, RADII), F32),
            vmem((8, ROWS, RADII), F32),
            vmem((4, 16, RADII), F32),
            vmem((8, COLS + 2, ROWS, RADII), F32),
            dma((4,)), dma((EARLY,)), dma((COLAT,)), dma((2,)), dma((2,)),
            dma((CHIPS,)), dma((CHIPS,)), dma((4,)), dma((CHIPS,)),
            dma((1,)), dma((EARLY,)), dma((1,)), dma((8,)), dma((1,)), dma((4,)), dma((4,)), dma((4,)),
            pltpu.SemaphoreType.REGULAR,
        ],
        compiler_params=pltpu.CompilerParams(collective_id=0, has_side_effects=True),
        cost_estimate=pl.CostEstimate(flops=30_000_000, bytes_accessed=2_000_000, transcendentals=0),
    )(jnp.transpose(fields[0], (0, 2, 1, 3)), donor_cell, target_slot, donor_frac)
    increment, sectioned = pl.pallas_call(
        write,
        out_shape=(shape, shape),
        in_specs=[pl.BlockSpec(memory_space=pltpu.VMEM)] * 2,
        out_specs=(hbm, hbm),
        scratch_shapes=[dma((2,))],
    )(pltpu.with_memory_space_constraint(increment, pltpu.VMEM), pltpu.with_memory_space_constraint(sectioned, pltpu.VMEM))
    return tuple(jnp.transpose(x, (0, 2, 1, 3))[None] for x in (increment, sectioned))


def solution(mesh):
    placed = (
        P("panel", None, "colat", "lon", None),
        P("panel", "colat", "lon"),
        P("panel", "colat", "lon"),
        P("panel", None, "colat", "lon"),
    )
    return jax.shard_map(
        shards,
        mesh=mesh,
        in_specs=placed,
        out_specs=(P("panel", None, "colat", "lon", None), P("panel", None, "colat", "lon", None)),
        check_vma=False,
    )
```
